32 devices in a mesh: groups: 2 (over y), seq: 4 (over z), head: 2 (over x), pair: 2 (over core).
Axes of the slice: x: 2, y: 2, z: 4, core: 2. Of those that a mesh axis runs over, the one named last changes fastest.
Arguments:
- query_rows: bfloat16 [2048, 1024], P(('groups', 'seq'), ('head', 'pair')), parts along dimension 0, may hold values from -6 to 6
- key_rows: bfloat16 [2048, 1024], P(('groups', 'seq'), ('head', 'pair')), parts along dimension 0, may hold values from -6 to 6
- value_rows: bfloat16 [2048, 1024], P(('groups', 'seq'), ('head', 'pair')), parts along dimension 0, may hold values from -6 to 6
- out_grad: bfloat16 [2048, 1024], P(('groups', 'seq'), ('head', 'pair')), parts along dimension 0, may hold values from -6 to 6
- random_blocks: int32 [32, 16, 3], P(('groups', 'head', 'pair'), 'seq'), parts along dimension 0, may hold values from 0 to 15, as said below
- global_positions: int32 [256], P('groups'), parts along dimension 0, may hold values from 0 to 1023, as said below
Outputs:
- attended: bfloat16 [2048, 1024], P(('groups', 'seq'), ('head', 'pair')), parts along dimension 0
- grad_query: bfloat16 [2048, 1024], P(('groups', 'seq'), ('head', 'pair')), parts along dimension 0
- grad_key: bfloat16 [2048, 1024], P(('groups', 'seq'), ('head', 'pair')), parts along dimension 0
- grad_value: bfloat16 [2048, 1024], P(('groups', 'seq'), ('head', 'pair')), parts along dimension 0
The draws below stay inside these ranges and needn't reach their ends.
There are 2 independent parts, one for each index of `groups`. The reference program is written for one: setup_inputs(seed, part) draws one part's arguments, and reference() takes and returns one part's arrays. A program takes and returns all parts, laid end to end along the dimension named above; each array names one. Nothing has to cross between parts.
Inputs may be any that keep to these rules, and one draw needn't show every extreme that they name: `random_blocks`: A query block's 3 random blocks are distinct, lie on another index of seq than the block itself (indices of seq hold 4 blocks each) and never in its window. For each head, the random blocks of the 4 query blocks of one index of seq take at most 4 blocks from any one index of seq, and this most is reached. `global_positions`: 128 distinct positions in increasing order.
All inputs are finite; a program needn't handle non-finite values.
Results may differ from the reference program's by a relative error of at most 0.0096.
The reference program's roundings to bfloat16 on the way count: a program that leaves them out, or rounds other values in their place, can miss the bound.
Values may be sent and summed in bfloat16 or wider, within the bound.
A program may use at most 64 MiB of HBM per device.

```python
import math
from functools import partial
import jax
import jax.numpy as jnp
from jax import lax

HEADS = 16
HD = 64
BLK = 64
RAND = 3
G = 128
SEQ = 1024
QB = 4
NB = 16


def pick_globals(key):
    order = jax.random.permutation(jax.random.fold_in(key, 11), SEQ)
    return jnp.sort(order[:G]).astype(jnp.int32)


def position_share():
    return (jnp.arange(SEQ, dtype=jnp.float32) + 0.5) / jnp.float32(SEQ)


def draw_global_positions(key, part):
    return pick_globals(key)


def draw_query_rows(key, part):
    base = jnp.clip(jax.random.normal(jax.random.fold_in(key, 31), (SEQ, HEADS * HD), jnp.float32), -6.0, 6.0)
    return base.astype(jnp.bfloat16)


def draw_key_rows(key, part):
    share = position_share()
    base = jax.random.normal(jax.random.fold_in(key, 32), (SEQ, HEADS * HD), jnp.float32)
    base = jnp.clip(base * (0.6 * jnp.power(3.0, share))[:, None], -6.0, 6.0)
    return base.astype(jnp.bfloat16)


def draw_value_rows(key, part):
    share = position_share()
    signs = jnp.where(jax.random.bernoulli(jax.random.fold_in(key, 52), 0.5, (HEADS * HD,)), 1.0, -1.0)
    noise = jax.random.normal(jax.random.fold_in(key, 51), (SEQ, HEADS * HD), jnp.float32)
    level = 1.2 * (2.0 * share - 1.0)
    base = jnp.clip(noise + level[:, None] * signs[None, :], -6.0, 6.0)
    return base.astype(jnp.bfloat16)


def draw_random_blocks(key, part):
    devices = NB // QB
    spread = devices - 1
    head_keys = jax.random.split(jax.random.fold_in(key, 41), HEADS * devices)
    orders = jax.vmap(lambda single: jax.random.permutation(single, QB))(head_keys).reshape(HEADS, devices, QB)
    starts = jax.random.randint(jax.random.fold_in(key, 44), (HEADS, devices, 1, 1), 0, spread)
    values = (orders[..., None] + starts + jnp.arange(RAND)[None, None, None, :]) % spread
    place = jnp.arange(devices)[None, :, None, None]
    owner = (place + 1 + values) % devices
    column = jnp.arange(QB)[None, None, :, None]
    low_bad = (owner == place - 1) & (column == 0)
    high_bad = (owner == place + 1) & (column == QB - 1)
    narrow = jax.random.randint(jax.random.fold_in(key, 42), owner.shape, 0, QB - 1)
    broad = jax.random.randint(jax.random.fold_in(key, 43), owner.shape, 0, QB)
    local = jnp.where(low_bad, narrow, jnp.where(high_bad, narrow + 1, broad))
    return (owner * QB + local).reshape(HEADS, NB, RAND).astype(jnp.int32)


def levels(own_key, dims, cuts, smallest, largest):
    gain, own = 1.0, jax.random.fold_in(own_key, 6)
    for position, blocks in cuts:
        steps = jnp.exp(jax.random.uniform(jax.random.fold_in(own, position), (blocks,), jnp.float32, smallest / len(cuts), largest / len(cuts)))
        gain = gain * jnp.repeat(steps, dims[position] // blocks).reshape([-1 if axis == position else 1 for axis in range(len(dims))])
    return gain


def scatter_about(key, dims, deviation, most, cuts=(), held_as=jnp.bfloat16):
    array = deviation * jax.random.normal(key, dims, jnp.float32)
    if cuts:
        array = array * levels(key, dims, cuts, -0.22, 0.18)
    return jnp.clip(array, -most, most).astype(held_as)


def setup_inputs(seed: int = 0, part: int = 0) -> dict:
    arg_keys = jax.random.split(jax.random.key(seed), 7)
    own_keys = jax.random.split(jax.random.fold_in(arg_keys[6], part), 7)
    return {
        "query_rows": draw_query_rows(jax.random.fold_in(jax.random.fold_in(arg_keys[6], part), 71), part),
        "key_rows": draw_key_rows(jax.random.fold_in(jax.random.fold_in(arg_keys[6], part), 71), part),
        "value_rows": draw_value_rows(jax.random.fold_in(jax.random.fold_in(arg_keys[6], part), 71), part),
        "out_grad": scatter_about(own_keys[3], (SEQ, HEADS * HD), 1.0, 6.0, ((0, 4), (1, 4))),
        "random_blocks": draw_random_blocks(jax.random.fold_in(jax.random.fold_in(arg_keys[6], part), 71), part),
        "global_positions": draw_global_positions(jax.random.fold_in(jax.random.fold_in(arg_keys[6], part), 71), part),
    }


def softmax_rows(scores):
    top = lax.optimization_barrier(jnp.max(scores, axis=-1, keepdims=True))
    raised = jnp.exp(scores - top)
    return raised / lax.optimization_barrier(jnp.sum(raised, axis=-1, keepdims=True))

def rounded(values):
    return lax.optimization_barrier(values.astype(jnp.bfloat16)).astype(jnp.float32)

def fold_window(parts):
    count = parts.shape[0]
    split = parts.reshape(count, 3, BLK, HD)
    padded = jnp.zeros((count + 2, BLK, HD), parts.dtype)
    padded = padded.at[0:count].add(split[:, 0]).at[1:count + 1].add(split[:, 1]).at[2:count + 2].add(split[:, 2])
    return padded[1:-1].reshape(count * BLK, HD)

def one_head(items, global_positions):
    query_head, key_head, value_head, grad_head, random_head = items
    scale = 1.0 / math.sqrt(HD)
    is_global = jnp.zeros((SEQ,), jnp.int32).at[global_positions].set(1) > 0
    global_block = global_positions // BLK
    block_ids = jnp.arange(NB)
    query_blocks = query_head.reshape(NB, BLK, HD).astype(jnp.float32)
    key_blocks = key_head.reshape(NB, BLK, HD).astype(jnp.float32)
    value_blocks = value_head.reshape(NB, BLK, HD).astype(jnp.float32)
    empty = jnp.zeros((1, BLK, HD), jnp.float32)
    key_pad = jnp.concatenate([empty, key_blocks, empty], axis=0)
    value_pad = jnp.concatenate([empty, value_blocks, empty], axis=0)
    window_keys = jnp.concatenate([key_pad[:-2], key_pad[1:-1], key_pad[2:]], axis=1)
    window_values = jnp.concatenate([value_pad[:-2], value_pad[1:-1], value_pad[2:]], axis=1)
    offset = jnp.repeat(jnp.arange(3), BLK) - 1
    neighbour = block_ids[:, None] + offset[None, :]
    window_valid = (neighbour >= 0) & (neighbour < NB)
    far_keys = key_blocks[random_head].reshape(NB, RAND * BLK, HD)
    far_values = value_blocks[random_head].reshape(NB, RAND * BLK, HD)
    glob_keys = key_head[global_positions].astype(jnp.float32)
    glob_values = value_head[global_positions].astype(jnp.float32)
    near_glob = jnp.abs(global_block[None, :] - block_ids[:, None]) <= 1
    in_random = jnp.any(random_head[:, :, None] == global_block[None, None, :], axis=1)
    global_keep = jnp.logical_not(near_glob | in_random)
    near = jnp.where(window_valid[:, None, :], jnp.einsum('bid,bjd->bij', query_blocks, window_keys) * scale, -jnp.inf)
    far = jnp.einsum('bid,bjd->bij', query_blocks, far_keys) * scale
    wide = jnp.where(global_keep[:, None, :], jnp.einsum('bid,gd->big', query_blocks, glob_keys) * scale, -jnp.inf)
    probs = softmax_rows(jnp.concatenate([near, far, wide], axis=-1))
    weights = rounded(probs)
    span = 3 * BLK
    reach = RAND * BLK
    sparse_out = jnp.einsum('bij,bjd->bid', weights[..., :span], window_values)
    sparse_out = sparse_out + jnp.einsum('bij,bjd->bid', weights[..., span:span + reach], far_values)
    sparse_out = sparse_out + jnp.einsum('big,gd->bid', weights[..., span + reach:], glob_values)
    sparse_out = sparse_out.reshape(SEQ, HD)
    glob_query = query_head[global_positions]
    glob_scores = jnp.dot(glob_query, key_head.T, preferred_element_type=jnp.float32) * scale
    glob_probs = softmax_rows(glob_scores)
    glob_weights = glob_probs.astype(jnp.bfloat16)
    glob_out = jnp.dot(glob_weights, value_head, preferred_element_type=jnp.float32)
    attended = sparse_out.at[global_positions].set(glob_out).astype(jnp.bfloat16)
    sparse_grad = jnp.where(is_global[:, None], jnp.zeros_like(grad_head), grad_head)
    delta = lax.optimization_barrier(jnp.sum(sparse_grad.astype(jnp.float32) * attended.astype(jnp.float32), axis=-1))
    grad_blocks = sparse_grad.reshape(NB, BLK, HD).astype(jnp.float32)
    value_dot = jnp.concatenate([jnp.einsum('bid,bjd->bij', grad_blocks, window_values), jnp.einsum('bid,bjd->bij', grad_blocks, far_values), jnp.einsum('bid,gd->big', grad_blocks, glob_values)], axis=-1)
    dscore = rounded(probs * (value_dot - delta.reshape(NB, BLK)[:, :, None]))
    grad_query = jnp.einsum('bij,bjd->bid', dscore[..., :span], window_keys)
    grad_query = grad_query + jnp.einsum('bij,bjd->bid', dscore[..., span:span + reach], far_keys)
    grad_query = grad_query + jnp.einsum('big,gd->bid', dscore[..., span + reach:], glob_keys)
    grad_query = (scale * grad_query).reshape(SEQ, HD)
    key_window = fold_window(scale * jnp.einsum('bij,bid->bjd', dscore[..., :span], query_blocks))
    value_window = fold_window(jnp.einsum('bij,bid->bjd', weights[..., :span], grad_blocks))
    key_far = rounded(scale * jnp.einsum('bij,bid->bjd', dscore[..., span:span + reach], query_blocks))
    value_far = rounded(jnp.einsum('bij,bid->bjd', weights[..., span:span + reach], grad_blocks))
    key_far_sum = jnp.zeros((NB, BLK, HD), jnp.float32).at[random_head].add(key_far.reshape(NB, RAND, BLK, HD)).reshape(SEQ, HD)
    value_far_sum = jnp.zeros((NB, BLK, HD), jnp.float32).at[random_head].add(value_far.reshape(NB, RAND, BLK, HD)).reshape(SEQ, HD)
    key_glob = scale * jnp.einsum('big,bid->gd', dscore[..., span + reach:], query_blocks)
    value_glob = jnp.einsum('big,bid->gd', weights[..., span + reach:], grad_blocks)
    glob_grad = grad_head[global_positions]
    glob_delta = lax.optimization_barrier(jnp.sum(glob_grad.astype(jnp.float32) * attended[global_positions].astype(jnp.float32), axis=-1))
    glob_dot = jnp.dot(glob_grad, value_head.T, preferred_element_type=jnp.float32)
    glob_dscore = (glob_probs * (glob_dot - glob_delta[:, None])).astype(jnp.bfloat16)
    grad_query = grad_query.at[global_positions].add(scale * jnp.dot(glob_dscore, key_head, preferred_element_type=jnp.float32))
    grad_key = key_window + key_far_sum + scale * jnp.dot(glob_dscore.T, glob_query, preferred_element_type=jnp.float32)
    grad_key = grad_key.at[global_positions].add(key_glob)
    grad_value = value_window + value_far_sum + jnp.dot(glob_weights.T, glob_grad, preferred_element_type=jnp.float32)
    grad_value = grad_value.at[global_positions].add(value_glob)
    return (attended, grad_query.astype(jnp.bfloat16), grad_key.astype(jnp.bfloat16), grad_value.astype(jnp.bfloat16))

def heads_first(rows):
    return jnp.transpose(rows.reshape(SEQ, HEADS, HD), (1, 0, 2))

def rows_back(stack):
    return jnp.transpose(stack, (1, 0, 2)).reshape(SEQ, HEADS * HD)

def reference(query_rows, key_rows, value_rows, out_grad, random_blocks, global_positions):
    results = lax.map(partial(one_head, global_positions=global_positions), (heads_first(query_rows), heads_first(key_rows), heads_first(value_rows), heads_first(out_grad), random_blocks))
    return (rows_back(results[0]), rows_back(results[1]), rows_back(results[2]), rows_back(results[3]))
```

```python
from functools import partial
import math

import jax
import jax.numpy as jnp
from jax import lax
from jax.experimental import pallas as pl
from jax.experimental.pallas import tpu as pltpu
from jax.sharding import PartitionSpec as P

HD = 64
BLK = 64
RAND = 3


def padded_2(array, sides, width):
    for axis, dim in sides:
        peers, length = (lax.axis_size(axis), array.shape[dim])
        up = [(i, (i + 1) % peers) for i in range(peers - 1)]
        down = [(j, i) for i, j in up]
        last = lax.slice_in_dim(array, length - width, length, axis=dim)
        leading = lax.slice_in_dim(array, 0, width, axis=dim)
        before = lax.ppermute(last, axis, up)
        after = lax.ppermute(leading, axis, down)
        array = jnp.concatenate([before, array, after], axis=dim)
    return array


def from_behind(array, axis, by):
    peers = lax.axis_size(axis)
    pairs = [(i, i + by) for i in range(peers) if 0 <= i + by < peers]
    return lax.ppermute(array, axis, pairs)


def softmax_rows(scores):
    top = jnp.max(scores, axis=-1, keepdims=True)
    raised = jnp.exp(scores - top)
    return raised / jnp.sum(raised, axis=-1, keepdims=True)


def group_probs(query, window, far_rows, global_rows, window_valid, global_keep, scale):
    near = (
        jnp.einsum("bihd,bjhd->bhij", query, window[..., :HD], preferred_element_type=jnp.float32)
        * scale
    )
    far = (
        jnp.einsum("bihd,bjhd->bhij", query, far_rows[..., :HD], preferred_element_type=jnp.float32)
        * scale
    )
    wide = (
        jnp.einsum(
            "bihd,jhd->bhij", query, global_rows[..., :HD], preferred_element_type=jnp.float32
        )
        * scale
    )
    near = jnp.where(window_valid[:, None, None, :], near, -jnp.inf)
    wide = jnp.where(global_keep[:, :, None, :], wide, -jnp.inf)
    return softmax_rows(jnp.concatenate([near, far, wide], axis=-1))


def split_keys(values, window, far_rows):
    span = window.shape[1]
    reach = far_rows.shape[1]
    return (values[..., :span], values[..., span : span + reach], values[..., span + reach :])


def forward_group(items, global_rows, scale):
    query, window, far_rows, window_valid, global_keep = items
    weights = group_probs(
        query, window, far_rows, global_rows, window_valid, global_keep, scale
    ).astype(jnp.bfloat16)
    near, far, wide = split_keys(weights, window, far_rows)
    out = jnp.einsum("bhij,bjhd->bihd", near, window[..., HD:], preferred_element_type=jnp.float32)
    out = out + jnp.einsum(
        "bhij,bjhd->bihd", far, far_rows[..., HD:], preferred_element_type=jnp.float32
    )
    return out + jnp.einsum(
        "bhij,jhd->bihd", wide, global_rows[..., HD:], preferred_element_type=jnp.float32
    )


def backward_group(items, global_rows, scale):
    query, window, far_rows, window_valid, global_keep, grad_out, delta = items
    probs = group_probs(query, window, far_rows, global_rows, window_valid, global_keep, scale)
    weights = probs.astype(jnp.bfloat16)
    value_dot = jnp.concatenate(
        [
            jnp.einsum(
                "bihd,bjhd->bhij", grad_out, window[..., HD:], preferred_element_type=jnp.float32
            ),
            jnp.einsum(
                "bihd,bjhd->bhij", grad_out, far_rows[..., HD:], preferred_element_type=jnp.float32
            ),
            jnp.einsum(
                "bihd,jhd->bhij",
                grad_out,
                global_rows[..., HD:],
                preferred_element_type=jnp.float32,
            ),
        ],
        axis=-1,
    )
    dscore = (probs * (value_dot - jnp.transpose(delta, (0, 2, 1))[..., None])).astype(jnp.bfloat16)
    dnear, dfar, dwide = split_keys(dscore, window, far_rows)
    near, far, wide = split_keys(weights, window, far_rows)
    grad_query = jnp.einsum(
        "bhij,bjhd->bihd", dnear, window[..., :HD], preferred_element_type=jnp.float32
    )
    grad_query = grad_query + jnp.einsum(
        "bhij,bjhd->bihd", dfar, far_rows[..., :HD], preferred_element_type=jnp.float32
    )
    grad_query = scale * (
        grad_query
        + jnp.einsum(
            "bhij,jhd->bihd", dwide, global_rows[..., :HD], preferred_element_type=jnp.float32
        )
    )
    grad_window = jnp.concatenate(
        [
            scale * jnp.einsum("bhij,bihd->bjhd", dnear, query, preferred_element_type=jnp.float32),
            jnp.einsum("bhij,bihd->bjhd", near, grad_out, preferred_element_type=jnp.float32),
        ],
        axis=-1,
    )
    grad_far = jnp.concatenate(
        [
            scale * jnp.einsum("bhij,bihd->bjhd", dfar, query, preferred_element_type=jnp.float32),
            jnp.einsum("bhij,bihd->bjhd", far, grad_out, preferred_element_type=jnp.float32),
        ],
        axis=-1,
    ).astype(jnp.bfloat16)
    grad_wide = jnp.concatenate(
        [
            scale * jnp.einsum("bhij,bihd->jhd", dwide, query, preferred_element_type=jnp.float32),
            jnp.einsum("bhij,bihd->jhd", wide, grad_out, preferred_element_type=jnp.float32),
        ],
        axis=-1,
    )
    return (grad_query, grad_window, grad_far, grad_wide)


def local_wide(query_rows, key_rows, value_rows, out_grad, random_blocks, global_positions):
    tokens = query_rows.shape[0]
    heads = query_rows.shape[1] // HD
    blocks = tokens // BLK
    devices = lax.axis_size("seq")
    place = lax.axis_index("seq")
    scale = 1.0 / math.sqrt(HD)
    capacity = RAND * (blocks // (devices - 1)) + min(RAND, blocks % (devices - 1))
    group = math.gcd(blocks, max(1, 512 // BLK))
    count = blocks // group
    local_index = global_positions - place * tokens
    owned = (local_index >= 0) & (local_index < tokens)
    target = jnp.where(owned, local_index, tokens)
    safe_index = jnp.where(owned, local_index, 0)

    def pick(rows):
        return jnp.where(owned[:, None], rows[safe_index].astype(jnp.float32), 0.0)

    glob_sum = (
        lax.psum(pick(query_rows).astype(jnp.bfloat16), "seq").astype(jnp.float32),
        lax.psum(pick(key_rows).astype(jnp.bfloat16), "seq").astype(jnp.float32),
        lax.psum(pick(value_rows).astype(jnp.bfloat16), "seq").astype(jnp.float32),
        lax.psum(pick(out_grad).astype(jnp.bfloat16), "seq").astype(jnp.float32),
    )
    glob_query = glob_sum[0].astype(jnp.bfloat16).reshape(-1, heads, HD)
    glob_key = glob_sum[1].astype(jnp.bfloat16).reshape(-1, heads, HD)
    glob_value = glob_sum[2].astype(jnp.bfloat16).reshape(-1, heads, HD)
    glob_grad = glob_sum[3].astype(jnp.bfloat16).reshape(-1, heads, HD)
    global_rows = jnp.concatenate([glob_key, glob_value], axis=-1)
    query3 = query_rows.reshape(tokens, heads, HD)
    key3 = key_rows.reshape(tokens, heads, HD)
    value3 = value_rows.reshape(tokens, heads, HD)
    pair_rows = jnp.concatenate([key3, value3], axis=-1)
    padded = padded_2(pair_rows, (("seq", 0),), BLK)
    framed = padded.reshape(blocks + 2, BLK, heads, 2 * HD)
    window = jnp.concatenate([framed[:-2], framed[1:-1], framed[2:]], axis=1)
    block_ids = place * blocks + jnp.arange(blocks)
    neighbour = block_ids[:, None] + (jnp.repeat(jnp.arange(3), BLK) - 1)[None, :]
    window_valid = (neighbour >= 0) & (neighbour < devices * blocks)
    global_block = global_positions // BLK
    near_glob = jnp.abs(global_block[None, :] - block_ids[:, None]) <= 1
    in_random = jnp.any(random_blocks[:, :, :, None] == global_block[None, None, None, :], axis=2)
    global_keep = jnp.logical_not(near_glob[:, None, :] | jnp.transpose(in_random, (1, 0, 2)))
    owner = random_blocks // blocks
    local_block = random_blocks % blocks
    flat_owner = owner.reshape(heads, blocks * RAND)
    hits = (flat_owner[:, :, None] == jnp.arange(devices)[None, None, :]).astype(jnp.int32)
    before = jnp.cumsum(hits, axis=1) - hits
    flat_slot = jnp.sum(before * hits, axis=2)
    placed = (flat_slot[:, :, None] == jnp.arange(capacity)[None, None, :]).astype(jnp.int32)
    marks = (local_block.reshape(heads, blocks * RAND) + 1)[:, :, None, None]
    table = jnp.sum(hits[:, :, :, None] * placed[:, :, None, :] * marks, axis=1) - 1
    asked = lax.all_to_all(
        jnp.transpose(table, (1, 0, 2)), "seq", split_axis=0, concat_axis=0, tiled=True
    )
    own_blocks = pair_rows.reshape(blocks, BLK, heads, 2 * HD)
    wanted = (jnp.maximum(asked, 0)[..., None] == jnp.arange(blocks)).astype(jnp.bfloat16)
    served = jnp.einsum(
        "zhcb,bthf->zhctf", wanted, own_blocks, preferred_element_type=jnp.float32
    ).astype(jnp.bfloat16)
    owner_order = jnp.transpose(owner, (1, 2, 0))
    slot_order = jnp.transpose(flat_slot.reshape(heads, blocks, RAND), (1, 2, 0))
    head_order = jnp.arange(heads)[None, None, :]
    arrived = lax.all_to_all(served, "seq", split_axis=0, concat_axis=0, tiled=True)
    arrived = jnp.transpose(arrived, (0, 2, 1, 3, 4)).reshape(
        devices * capacity, heads, BLK, 2 * HD
    )
    source = owner_order * capacity + slot_order
    chosen = (source[..., None] == jnp.arange(devices * capacity)).astype(jnp.bfloat16)
    picked = jnp.einsum(
        "brhz,zhtf->brhtf", chosen, arrived, preferred_element_type=jnp.float32
    ).astype(jnp.bfloat16)
    far_rows = jnp.transpose(picked, (0, 1, 3, 2, 4)).reshape(blocks, RAND * BLK, heads, 2 * HD)

    def grouped(array):
        return array.reshape((count, group) + array.shape[1:])

    query_blocks = query3.reshape(blocks, BLK, heads, HD)
    sparse_out = lax.map(
        partial(forward_group, global_rows=global_rows, scale=scale),
        (
            grouped(query_blocks),
            grouped(window),
            grouped(far_rows),
            grouped(window_valid),
            grouped(global_keep),
        ),
    )
    sparse_out = sparse_out.reshape(tokens, heads, HD)
    wide = jnp.einsum("ghd,thd->hgt", glob_query, key3, preferred_element_type=jnp.float32) * scale
    local_top = jnp.max(wide, axis=-1)
    top = lax.pmax(local_top, "seq")
    total = lax.psum(jnp.sum(jnp.exp(wide - top[..., None]), axis=-1), "seq")
    glob_probs = jnp.exp(wide - top[..., None]) / total[..., None]
    glob_weights = glob_probs.astype(jnp.bfloat16)
    glob_part = jnp.einsum("hgt,thd->ghd", glob_weights, value3, preferred_element_type=jnp.float32)
    glob_out = lax.psum(glob_part, "seq").astype(jnp.bfloat16)
    attended = sparse_out.astype(jnp.bfloat16).at[target].set(glob_out, mode="drop")
    glob_mask = jnp.zeros((tokens,), jnp.bool_).at[target].set(True, mode="drop")
    sparse_grad = jnp.where(
        glob_mask[:, None, None],
        jnp.zeros_like(out_grad.reshape(tokens, heads, HD)),
        out_grad.reshape(tokens, heads, HD),
    )
    delta = jnp.sum(sparse_grad.astype(jnp.float32) * attended.astype(jnp.float32), axis=-1)
    grad_query, grad_window, grad_far, grad_wide = lax.map(
        partial(backward_group, global_rows=global_rows, scale=scale),
        (
            grouped(query_blocks),
            grouped(window),
            grouped(far_rows),
            grouped(window_valid),
            grouped(global_keep),
            grouped(sparse_grad.reshape(blocks, BLK, heads, HD)),
            grouped(delta.reshape(blocks, BLK, heads)),
        ),
    )
    grad_query = grad_query.reshape(tokens, heads, HD)
    grad_window = grad_window.reshape(blocks, 3, BLK, heads, 2 * HD)
    grad_wide = jnp.sum(grad_wide, axis=0)
    folded = jnp.zeros((blocks + 2, BLK, heads, 2 * HD), jnp.float32)
    folded = (
        folded.at[0:blocks]
        .add(grad_window[:, 0])
        .at[1 : blocks + 1]
        .add(grad_window[:, 1])
        .at[2 : blocks + 2]
        .add(grad_window[:, 2])
    )
    from_right = from_behind(folded[0], "seq", -1)
    from_left = from_behind(folded[blocks + 1], "seq", 1)
    local_pair = folded[1 : blocks + 1]
    local_pair = local_pair.at[blocks - 1].add(from_right).at[0].add(from_left)
    far_terms = jnp.transpose(grad_far.reshape(blocks, RAND, BLK, heads, 2 * HD), (0, 1, 3, 2, 4))
    outgoing = (
        jnp.zeros((devices, heads, capacity, BLK, 2 * HD), jnp.bfloat16)
        .at[owner_order, head_order, slot_order]
        .set(far_terms)
    )
    returned = lax.all_to_all(outgoing, "seq", split_axis=0, concat_axis=0, tiled=True)
    landing = jnp.where(asked >= 0, asked, blocks)
    gathered = (
        jnp.zeros((blocks, heads, BLK, 2 * HD), jnp.float32)
        .at[landing, jnp.arange(heads)[None, :, None]]
        .add(returned.astype(jnp.float32), mode="drop")
    )
    pair_grad = local_pair.reshape(tokens, heads, 2 * HD) + jnp.transpose(
        gathered, (0, 2, 1, 3)
    ).reshape(tokens, heads, 2 * HD)
    glob_attended = glob_out.astype(jnp.float32)
    glob_delta = jnp.sum(glob_grad.astype(jnp.float32) * glob_attended, axis=-1)
    glob_dot = jnp.einsum("ghd,thd->hgt", glob_grad, value3, preferred_element_type=jnp.float32)
    glob_dscore = (glob_probs * (glob_dot - jnp.transpose(glob_delta)[..., None])).astype(
        jnp.bfloat16
    )
    query_part = scale * jnp.einsum(
        "hgt,thd->ghd", glob_dscore, key3, preferred_element_type=jnp.float32
    )
    key_from_glob = scale * jnp.einsum(
        "hgt,ghd->thd", glob_dscore, glob_query, preferred_element_type=jnp.float32
    )
    value_from_glob = jnp.einsum(
        "hgt,ghd->thd", glob_weights, glob_grad, preferred_element_type=jnp.float32
    )
    summed = lax.psum((query_part, grad_wide), "seq")
    grad_query = grad_query.at[target].add(summed[0], mode="drop")
    pair_grad = pair_grad.at[target].add(summed[1], mode="drop")
    grad_key = pair_grad[..., :HD] + key_from_glob
    grad_value = pair_grad[..., HD:] + value_from_glob
    return (
        attended.reshape(tokens, heads * HD),
        grad_query.reshape(tokens, heads * HD).astype(jnp.bfloat16),
        grad_key.reshape(tokens, heads * HD).astype(jnp.bfloat16),
        grad_value.reshape(tokens, heads * HD).astype(jnp.bfloat16),
    )


BIG = 1e30
LIMIT = 63 * 1024 * 1024
NT = (((1,), (1,)), ((), ()))
TN = (((0,), (0,)), ((), ()))
NN = (((1,), (0,)), ((), ()))


def mm(left, right, dims):
    return lax.dot_general(left, right, dims, preferred_element_type=jnp.float32)


def head_kernel(
    n, tokens, q_hbm, k_hbm, v_hbm, g_hbm, rb_hbm, gp_hbm, att_ref, dq_ref, dk_ref, dv_ref,
    q_ref, k_ref, v_ref, g_ref, rb_ref, gp_ref, kq_send, vd_send, tab_send, kq, vd, tab, o1_send, o2_send, o1, o2,
    ka, qa, probs, weights, dscore, load_sem, send_sem, recv_sem,
):
    me = lax.axis_index("seq")
    total = n * tokens
    qb = tokens // BLK
    scale = 1.0 / math.sqrt(HD)
    peers = [lax.rem(me + off, n) for off in range(1, n)]
    sources = [lax.rem(me + n - off, n) for off in range(1, n)]

    loads = [
        pltpu.make_async_copy(hbm, vmem, load_sem.at[i])
        for i, (hbm, vmem) in enumerate(
            ((k_hbm, k_ref), (q_hbm, q_ref), (v_hbm, v_ref), (g_hbm, g_ref), (rb_hbm, rb_ref), (gp_hbm, gp_ref))
        )
    ]
    for load in loads:
        load.start()
    barrier = pltpu.get_barrier_semaphore()
    for peer in peers:
        pl.semaphore_signal(
            barrier, inc=1, device_id={"seq": peer}, device_id_type=pl.DeviceIdType.MESH
        )

    def copy(stage, off, send, recv, slot):
        return pltpu.make_async_remote_copy(
            src_ref=send.at[peers[off - 1]],
            dst_ref=recv.at[slot],
            send_sem=send_sem.at[stage, off - 1],
            recv_sem=recv_sem.at[stage, off - 1],
            device_id={"seq": peers[off - 1]},
            device_id_type=pl.DeviceIdType.MESH,
        )

    def start(stage, off, send, recv):
        copy(stage, off, send, recv, me).start()

    def arrive(stage, off, send, recv):
        copy(stage, off, send, recv, sources[off - 1]).wait_recv()

    row = lax.broadcasted_iota(jnp.int32, (8, 128), 0)
    lane = lax.broadcasted_iota(jnp.int32, (8, 128), 1)
    loads[4].wait()
    for h in range(n):
        mark = jnp.zeros((8, 128), jnp.float32)
        for b in range(qb):
            hit = lane == rb_ref[0, h, b]
            for r in range(1, RAND):
                hit = hit | (lane == rb_ref[r, h, b])
            mark = jnp.where(hit & (row == b), 1.0, mark)
        tab_send[h] = mark
    loads[0].wait()
    loads[1].wait()
    for h in range(n):
        cols = slice(h * HD, (h + 1) * HD)
        kq_send[h, :, 0:HD] = k_ref[:, cols]
        kq_send[h, :, HD : 2 * HD] = q_ref[:, cols] * jnp.bfloat16(scale)
    pl.semaphore_wait(barrier, n - 1)
    order = [2, 1, 3] if n == 4 else list(range(1, n))
    for off in order:
        start(0, off, tab_send, tab)
        start(1, off, kq_send, kq)
    loads[2].wait()
    loads[3].wait()
    for h in range(n):
        cols = slice(h * HD, (h + 1) * HD)
        vd_send[h, :, 0:HD] = v_ref[:, cols]
        vd_send[h, :, HD : 2 * HD] = g_ref[:, cols]
    for off in order:
        start(2, off, vd_send, vd)
    kq[me] = kq_send[me]
    vd[me] = vd_send[me]
    tab[me] = tab_send[me]

    pos = lax.broadcasted_iota(jnp.int32, (total, 128), 0)
    col = lax.broadcasted_iota(jnp.int32, (total, 128), 1)
    loads[5].wait()
    globals_here = gp_ref.shape[1]
    spots = lax.broadcasted_iota(jnp.int32, (total, globals_here), 0) == gp_ref[...]
    spread = mm(
        jnp.where(spots, 1.0, 0.0).astype(jnp.bfloat16),
        jnp.ones((globals_here, 128), jnp.bfloat16),
        NN,
    )
    is_global = spread > 0.5
    slot = col - HD
    block = (slot // 8) * qb + slot % 8
    mine = (slot >= 0) & (slot < 8 * n) & (slot % 8 < qb)
    key_block = pos // BLK
    near = mine & (block - key_block <= 1) & (key_block - block <= 1)
    open_key = near | is_global
    hot = jnp.where(mine & (block == key_block) & jnp.logical_not(is_global), 1.0, 0.0)
    place = jnp.where(col == key_block, 1.0, 0.0).astype(jnp.bfloat16)

    for off in order:
        arrive(0, off, tab_send, tab)
        arrive(1, off, kq_send, kq)
    table = jnp.concatenate(
        [
            jnp.zeros((HD, 128), jnp.float32),
            tab[...].reshape(8 * n, 128),
            jnp.zeros((128 - HD - 8 * n, 128), jnp.float32),
        ],
        axis=0,
    ).astype(jnp.bfloat16)
    chosen = mm(place, table, NT)
    bias = jnp.where(open_key | (chosen > 0.5), 0.0, -BIG).astype(jnp.bfloat16)
    pair = kq[...].reshape(total, 128)
    ka[...] = bias
    ka[:, 0:HD] = pair[:, 0:HD]
    qa[...] = hot.astype(jnp.bfloat16)
    qa[:, 0:HD] = pair[:, HD : 2 * HD]

    keys = ka[...]
    for a in range(n):
        rows = pl.ds(a * tokens, tokens)
        score = mm(keys, qa[rows, :], NT)
        top = jnp.max(score, axis=0, keepdims=True)
        raised = jnp.exp(score - top)
        prob = raised * (1.0 / jnp.sum(raised, axis=0, keepdims=True))
        probs[a] = prob
        weights[a] = prob.astype(jnp.bfloat16)

    for off in order:
        arrive(2, off, vd_send, vd)
    values = vd[...].reshape(total, 2 * HD)[:, 0:HD]
    values_t = values.T
    keys_t = keys[:, 0:HD].T
    steps = order + [0]
    deltas = []
    for off in steps:
        a = lax.rem(me + off, n)
        rows = pl.ds(pl.multiple_of(a * tokens, tokens), tokens)
        out = mm(values_t, weights[a], NN).T.astype(jnp.bfloat16)
        grad = vd[a, :, HD : 2 * HD]
        deltas.append(jnp.sum(grad.astype(jnp.float32).T * out.astype(jnp.float32).T, axis=0, keepdims=True))
        dv = jnp.zeros((tokens, HD), jnp.float32)
        for c in range(n):
            dv = dv + mm(weights[c, rows, :], vd[c, :, HD : 2 * HD], NN)
        o1_send[a, :, 0:HD] = out
        o1_send[a, :, HD : 2 * HD] = dv.astype(jnp.bfloat16)
        if off:
            start(3, off, o1_send, o1)
        else:
            o1[me] = o1_send[me]

    for step, off in enumerate(steps):
        a = lax.rem(me + off, n)
        dprob = mm(values, vd[a, :, HD : 2 * HD], NT)
        ds = (probs[a] * (dprob - deltas[step])).astype(jnp.bfloat16)
        dscore[a] = ds
        dq = mm(keys_t, ds, NN).T * scale
        o2_send[a, :, 0:HD] = dq.astype(jnp.bfloat16)
    for off in steps:
        a = lax.rem(me + off, n)
        rows = pl.ds(pl.multiple_of(a * tokens, tokens), tokens)
        dk = jnp.zeros((tokens, HD), jnp.float32)
        for c in range(n):
            dk = dk + mm(dscore[c, rows, :], qa[c * tokens : (c + 1) * tokens, 0:HD], NN)
        o2_send[a, :, HD : 2 * HD] = dk.astype(jnp.bfloat16)
        if off:
            start(4, off, o2_send, o2)
        else:
            o2[me] = o2_send[me]

    for off in order:
        arrive(3, off, o1_send, o1)
    for h in range(n):
        cols = slice(h * HD, (h + 1) * HD)
        att_ref[:, cols] = o1[h, :, 0:HD]
        dv_ref[:, cols] = o1[h, :, HD : 2 * HD]
    for off in order:
        arrive(4, off, o2_send, o2)
    for h in range(n):
        cols = slice(h * HD, (h + 1) * HD)
        dq_ref[:, cols] = o2[h, :, 0:HD]
        dk_ref[:, cols] = o2[h, :, HD : 2 * HD]
    for stage, (send, recv) in enumerate(
        ((tab_send, tab), (kq_send, kq), (vd_send, vd), (o1_send, o1), (o2_send, o2))
    ):
        for off in order:
            copy(stage, off, send, recv, me).wait_send()


def write_out(*refs):
    count = len(refs) // 2
    sources, targets, sem = refs[:count], refs[count : 2 * count], refs[-1]
    stores = [pltpu.make_async_copy(sources[i], targets[i], sem.at[i]) for i in range(count)]
    for store in stores:
        store.start()
    for store in stores:
        store.wait()


def local_heads(query_rows, key_rows, value_rows, out_grad, random_blocks, global_positions):
    tokens, width = query_rows.shape
    n = lax.axis_size("seq")
    total = n * tokens
    bf16, f32 = jnp.bfloat16, jnp.float32
    where_it_lies = pl.BlockSpec(memory_space=pltpu.HBM)
    rows = [pltpu.VMEM((tokens, width), bf16)] * 4
    part = pltpu.VMEM((n, tokens, 2 * HD), bf16)
    small = pltpu.VMEM((n, 8, 128), f32)
    results = pl.pallas_call(
        partial(head_kernel, n, tokens),
        out_shape=[pltpu.VMEM((tokens, width), bf16)] * 4,
        in_specs=[where_it_lies] * 6,
        out_specs=[pl.BlockSpec(memory_space=pltpu.VMEM)] * 4,
        scratch_shapes=[
            *rows, pltpu.SMEM((RAND,) + random_blocks.shape[:2], jnp.int32), pltpu.VMEM((1, global_positions.shape[0]), jnp.int32), part, part, small, part, part, small, part, part, part, part,
            pltpu.VMEM((total, 128), bf16),
            pltpu.VMEM((total, 128), bf16),
            pltpu.VMEM((n, total, tokens), f32),
            pltpu.VMEM((n, total, tokens), bf16),
            pltpu.VMEM((n, total, tokens), bf16),
            pltpu.SemaphoreType.DMA((6,)),
            pltpu.SemaphoreType.DMA((5, n - 1)),
            pltpu.SemaphoreType.DMA((5, n - 1)),
        ],
        compiler_params=pltpu.CompilerParams(
            collective_id=0, has_side_effects=True, vmem_limit_bytes=LIMIT
        ),
        cost_estimate=pl.CostEstimate(
            flops=14 * total * total * HD, bytes_accessed=16 * tokens * width, transcendentals=total * total
        ),
    )(
        query_rows, key_rows, value_rows, out_grad,
        jnp.transpose(random_blocks, (2, 0, 1)), global_positions.reshape(1, -1),
    )
    return pl.pallas_call(
        write_out,
        out_shape=[jax.ShapeDtypeStruct((tokens, width), bf16)] * 4,
        in_specs=[pl.BlockSpec(memory_space=pltpu.VMEM)] * 4,
        out_specs=[where_it_lies] * 4,
        scratch_shapes=[pltpu.SemaphoreType.DMA((4,))],
    )(*(pltpu.with_memory_space_constraint(r, pltpu.VMEM) for r in results))


def local(query_rows, key_rows, value_rows, out_grad, random_blocks, global_positions):
    n = lax.axis_size("seq")
    tokens = query_rows.shape[0]
    one_head_each = query_rows.shape[1] == n * HD and n > 1
    fits = 8 * n <= 128 - HD and tokens // BLK <= 8 and n * tokens // BLK <= 128
    if one_head_each and fits and tokens % 256 == 0 and n * tokens <= 1024:
        run = local_heads
    else:
        run = local_wide
    return run(query_rows, key_rows, value_rows, out_grad, random_blocks, global_positions)


def solution(mesh):
    placed = (
        P(("groups", "seq"), ("head", "pair")),
        P(("groups", "seq"), ("head", "pair")),
        P(("groups", "seq"), ("head", "pair")),
        P(("groups", "seq"), ("head", "pair")),
        P(("groups", "head", "pair"), "seq", None),
        P("groups"),
    )
    return jax.shard_map(
        local,
        mesh=mesh,
        in_specs=placed,
        out_specs=(
            P(("groups", "seq"), ("head", "pair")),
            P(("groups", "seq"), ("head", "pair")),
            P(("groups", "seq"), ("head", "pair")),
            P(("groups", "seq"), ("head", "pair")),
        ),
        check_vma=False,
    )
```

```python
from functools import partial
import math

import jax
import jax.numpy as jnp
from jax import lax
from jax.experimental import pallas as pl
from jax.experimental.pallas import tpu as pltpu
from jax.sharding import PartitionSpec as P

HD = 64
BLK = 64
RAND = 3


def padded_2(array, sides, width):
    for axis, dim in sides:
        peers, length = (lax.axis_size(axis), array.shape[dim])
        up = [(i, (i + 1) % peers) for i in range(peers - 1)]
        down = [(j, i) for i, j in up]
        last = lax.slice_in_dim(array, length - width, length, axis=dim)
        leading = lax.slice_in_dim(array, 0, width, axis=dim)
        before = lax.ppermute(last, axis, up)
        after = lax.ppermute(leading, axis, down)
        array = jnp.concatenate([before, array, after], axis=dim)
    return array


def from_behind(array, axis, by):
    peers = lax.axis_size(axis)
    pairs = [(i, i + by) for i in range(peers) if 0 <= i + by < peers]
    return lax.ppermute(array, axis, pairs)


def softmax_rows(scores):
    top = jnp.max(scores, axis=-1, keepdims=True)
    raised = jnp.exp(scores - top)
    return raised / jnp.sum(raised, axis=-1, keepdims=True)


def group_probs(query, window, far_rows, global_rows, window_valid, global_keep, scale):
    near = (
        jnp.einsum("bihd,bjhd->bhij", query, window[..., :HD], preferred_element_type=jnp.float32)
        * scale
    )
    far = (
        jnp.einsum("bihd,bjhd->bhij", query, far_rows[..., :HD], preferred_element_type=jnp.float32)
        * scale
    )
    wide = (
        jnp.einsum(
            "bihd,jhd->bhij", query, global_rows[..., :HD], preferred_element_type=jnp.float32
        )
        * scale
    )
    near = jnp.where(window_valid[:, None, None, :], near, -jnp.inf)
    wide = jnp.where(global_keep[:, :, None, :], wide, -jnp.inf)
    return softmax_rows(jnp.concatenate([near, far, wide], axis=-1))


def split_keys(values, window, far_rows):
    span = window.shape[1]
    reach = far_rows.shape[1]
    return (values[..., :span], values[..., span : span + reach], values[..., span + reach :])


def forward_group(items, global_rows, scale):
    query, window, far_rows, window_valid, global_keep = items
    weights = group_probs(
        query, window, far_rows, global_rows, window_valid, global_keep, scale
    ).astype(jnp.bfloat16)
    near, far, wide = split_keys(weights, window, far_rows)
    out = jnp.einsum("bhij,bjhd->bihd", near, window[..., HD:], preferred_element_type=jnp.float32)
    out = out + jnp.einsum(
        "bhij,bjhd->bihd", far, far_rows[..., HD:], preferred_element_type=jnp.float32
    )
    return out + jnp.einsum(
        "bhij,jhd->bihd", wide, global_rows[..., HD:], preferred_element_type=jnp.float32
    )


def backward_group(items, global_rows, scale):
    query, window, far_rows, window_valid, global_keep, grad_out, delta = items
    probs = group_probs(query, window, far_rows, global_rows, window_valid, global_keep, scale)
    weights = probs.astype(jnp.bfloat16)
    value_dot = jnp.concatenate(
        [
            jnp.einsum(
                "bihd,bjhd->bhij", grad_out, window[..., HD:], preferred_element_type=jnp.float32
            ),
            jnp.einsum(
                "bihd,bjhd->bhij", grad_out, far_rows[..., HD:], preferred_element_type=jnp.float32
            ),
            jnp.einsum(
                "bihd,jhd->bhij",
                grad_out,
                global_rows[..., HD:],
                preferred_element_type=jnp.float32,
            ),
        ],
        axis=-1,
    )
    dscore = (probs * (value_dot - jnp.transpose(delta, (0, 2, 1))[..., None])).astype(jnp.bfloat16)
    dnear, dfar, dwide = split_keys(dscore, window, far_rows)
    near, far, wide = split_keys(weights, window, far_rows)
    grad_query = jnp.einsum(
        "bhij,bjhd->bihd", dnear, window[..., :HD], preferred_element_type=jnp.float32
    )
    grad_query = grad_query + jnp.einsum(
        "bhij,bjhd->bihd", dfar, far_rows[..., :HD], preferred_element_type=jnp.float32
    )
    grad_query = scale * (
        grad_query
        + jnp.einsum(
            "bhij,jhd->bihd", dwide, global_rows[..., :HD], preferred_element_type=jnp.float32
        )
    )
    grad_window = jnp.concatenate(
        [
            scale * jnp.einsum("bhij,bihd->bjhd", dnear, query, preferred_element_type=jnp.float32),
            jnp.einsum("bhij,bihd->bjhd", near, grad_out, preferred_element_type=jnp.float32),
        ],
        axis=-1,
    )
    grad_far = jnp.concatenate(
        [
            scale * jnp.einsum("bhij,bihd->bjhd", dfar, query, preferred_element_type=jnp.float32),
            jnp.einsum("bhij,bihd->bjhd", far, grad_out, preferred_element_type=jnp.float32),
        ],
        axis=-1,
    ).astype(jnp.bfloat16)
    grad_wide = jnp.concatenate(
        [
            scale * jnp.einsum("bhij,bihd->jhd", dwide, query, preferred_element_type=jnp.float32),
            jnp.einsum("bhij,bihd->jhd", wide, grad_out, preferred_element_type=jnp.float32),
        ],
        axis=-1,
    )
    return (grad_query, grad_window, grad_far, grad_wide)


def local_wide(query_rows, key_rows, value_rows, out_grad, random_blocks, global_positions):
    tokens = query_rows.shape[0]
    heads = query_rows.shape[1] // HD
    blocks = tokens // BLK
    devices = lax.axis_size("seq")
    place = lax.axis_index("seq")
    scale = 1.0 / math.sqrt(HD)
    capacity = RAND * (blocks // (devices - 1)) + min(RAND, blocks % (devices - 1))
    group = math.gcd(blocks, max(1, 512 // BLK))
    count = blocks // group
    local_index = global_positions - place * tokens
    owned = (local_index >= 0) & (local_index < tokens)
    target = jnp.where(owned, local_index, tokens)
    safe_index = jnp.where(owned, local_index, 0)

    def pick(rows):
        return jnp.where(owned[:, None], rows[safe_index].astype(jnp.float32), 0.0)

    glob_sum = (
        lax.psum(pick(query_rows).astype(jnp.bfloat16), "seq").astype(jnp.float32),
        lax.psum(pick(key_rows).astype(jnp.bfloat16), "seq").astype(jnp.float32),
        lax.psum(pick(value_rows).astype(jnp.bfloat16), "seq").astype(jnp.float32),
        lax.psum(pick(out_grad).astype(jnp.bfloat16), "seq").astype(jnp.float32),
    )
    glob_query = glob_sum[0].astype(jnp.bfloat16).reshape(-1, heads, HD)
    glob_key = glob_sum[1].astype(jnp.bfloat16).reshape(-1, heads, HD)
    glob_value = glob_sum[2].astype(jnp.bfloat16).reshape(-1, heads, HD)
    glob_grad = glob_sum[3].astype(jnp.bfloat16).reshape(-1, heads, HD)
    global_rows = jnp.concatenate([glob_key, glob_value], axis=-1)
    query3 = query_rows.reshape(tokens, heads, HD)
    key3 = key_rows.reshape(tokens, heads, HD)
    value3 = value_rows.reshape(tokens, heads, HD)
    pair_rows = jnp.concatenate([key3, value3], axis=-1)
    padded = padded_2(pair_rows, (("seq", 0),), BLK)
    framed = padded.reshape(blocks + 2, BLK, heads, 2 * HD)
    window = jnp.concatenate([framed[:-2], framed[1:-1], framed[2:]], axis=1)
    block_ids = place * blocks + jnp.arange(blocks)
    neighbour = block_ids[:, None] + (jnp.repeat(jnp.arange(3), BLK) - 1)[None, :]
    window_valid = (neighbour >= 0) & (neighbour < devices * blocks)
    global_block = global_positions // BLK
    near_glob = jnp.abs(global_block[None, :] - block_ids[:, None]) <= 1
    in_random = jnp.any(random_blocks[:, :, :, None] == global_block[None, None, None, :], axis=2)
    global_keep = jnp.logical_not(near_glob[:, None, :] | jnp.transpose(in_random, (1, 0, 2)))
    owner = random_blocks // blocks
    local_block = random_blocks % blocks
    flat_owner = owner.reshape(heads, blocks * RAND)
    hits = (flat_owner[:, :, None] == jnp.arange(devices)[None, None, :]).astype(jnp.int32)
    before = jnp.cumsum(hits, axis=1) - hits
    flat_slot = jnp.sum(before * hits, axis=2)
    placed = (flat_slot[:, :, None] == jnp.arange(capacity)[None, None, :]).astype(jnp.int32)
    marks = (local_block.reshape(heads, blocks * RAND) + 1)[:, :, None, None]
    table = jnp.sum(hits[:, :, :, None] * placed[:, :, None, :] * marks, axis=1) - 1
    asked = lax.all_to_all(
        jnp.transpose(table, (1, 0, 2)), "seq", split_axis=0, concat_axis=0, tiled=True
    )
    own_blocks = pair_rows.reshape(blocks, BLK, heads, 2 * HD)
    wanted = (jnp.maximum(asked, 0)[..., None] == jnp.arange(blocks)).astype(jnp.bfloat16)
    served = jnp.einsum(
        "zhcb,bthf->zhctf", wanted, own_blocks, preferred_element_type=jnp.float32
    ).astype(jnp.bfloat16)
    owner_order = jnp.transpose(owner, (1, 2, 0))
    slot_order = jnp.transpose(flat_slot.reshape(heads, blocks, RAND), (1, 2, 0))
    head_order = jnp.arange(heads)[None, None, :]
    arrived = lax.all_to_all(served, "seq", split_axis=0, concat_axis=0, tiled=True)
    arrived = jnp.transpose(arrived, (0, 2, 1, 3, 4)).reshape(
        devices * capacity, heads, BLK, 2 * HD
    )
    source = owner_order * capacity + slot_order
    chosen = (source[..., None] == jnp.arange(devices * capacity)).astype(jnp.bfloat16)
    picked = jnp.einsum(
        "brhz,zhtf->brhtf", chosen, arrived, preferred_element_type=jnp.float32
    ).astype(jnp.bfloat16)
    far_rows = jnp.transpose(picked, (0, 1, 3, 2, 4)).reshape(blocks, RAND * BLK, heads, 2 * HD)

    def grouped(array):
        return array.reshape((count, group) + array.shape[1:])

    query_blocks = query3.reshape(blocks, BLK, heads, HD)
    sparse_out = lax.map(
        partial(forward_group, global_rows=global_rows, scale=scale),
        (
            grouped(query_blocks),
            grouped(window),
            grouped(far_rows),
            grouped(window_valid),
            grouped(global_keep),
        ),
    )
    sparse_out = sparse_out.reshape(tokens, heads, HD)
    wide = jnp.einsum("ghd,thd->hgt", glob_query, key3, preferred_element_type=jnp.float32) * scale
    local_top = jnp.max(wide, axis=-1)
    top = lax.pmax(local_top, "seq")
    total = lax.psum(jnp.sum(jnp.exp(wide - top[..., None]), axis=-1), "seq")
    glob_probs = jnp.exp(wide - top[..., None]) / total[..., None]
    glob_weights = glob_probs.astype(jnp.bfloat16)
    glob_part = jnp.einsum("hgt,thd->ghd", glob_weights, value3, preferred_element_type=jnp.float32)
    glob_out = lax.psum(glob_part, "seq").astype(jnp.bfloat16)
    attended = sparse_out.astype(jnp.bfloat16).at[target].set(glob_out, mode="drop")
    glob_mask = jnp.zeros((tokens,), jnp.bool_).at[target].set(True, mode="drop")
    sparse_grad = jnp.where(
        glob_mask[:, None, None],
        jnp.zeros_like(out_grad.reshape(tokens, heads, HD)),
        out_grad.reshape(tokens, heads, HD),
    )
    delta = jnp.sum(sparse_grad.astype(jnp.float32) * attended.astype(jnp.float32), axis=-1)
    grad_query, grad_window, grad_far, grad_wide = lax.map(
        partial(backward_group, global_rows=global_rows, scale=scale),
        (
            grouped(query_blocks),
            grouped(window),
            grouped(far_rows),
            grouped(window_valid),
            grouped(global_keep),
            grouped(sparse_grad.reshape(blocks, BLK, heads, HD)),
            grouped(delta.reshape(blocks, BLK, heads)),
        ),
    )
    grad_query = grad_query.reshape(tokens, heads, HD)
    grad_window = grad_window.reshape(blocks, 3, BLK, heads, 2 * HD)
    grad_wide = jnp.sum(grad_wide, axis=0)
    folded = jnp.zeros((blocks + 2, BLK, heads, 2 * HD), jnp.float32)
    folded = (
        folded.at[0:blocks]
        .add(grad_window[:, 0])
        .at[1 : blocks + 1]
        .add(grad_window[:, 1])
        .at[2 : blocks + 2]
        .add(grad_window[:, 2])
    )
    from_right = from_behind(folded[0], "seq", -1)
    from_left = from_behind(folded[blocks + 1], "seq", 1)
    local_pair = folded[1 : blocks + 1]
    local_pair = local_pair.at[blocks - 1].add(from_right).at[0].add(from_left)
    far_terms = jnp.transpose(grad_far.reshape(blocks, RAND, BLK, heads, 2 * HD), (0, 1, 3, 2, 4))
    outgoing = (
        jnp.zeros((devices, heads, capacity, BLK, 2 * HD), jnp.bfloat16)
        .at[owner_order, head_order, slot_order]
        .set(far_terms)
    )
    returned = lax.all_to_all(outgoing, "seq", split_axis=0, concat_axis=0, tiled=True)
    landing = jnp.where(asked >= 0, asked, blocks)
    gathered = (
        jnp.zeros((blocks, heads, BLK, 2 * HD), jnp.float32)
        .at[landing, jnp.arange(heads)[None, :, None]]
        .add(returned.astype(jnp.float32), mode="drop")
    )
    pair_grad = local_pair.reshape(tokens, heads, 2 * HD) + jnp.transpose(
        gathered, (0, 2, 1, 3)
    ).reshape(tokens, heads, 2 * HD)
    glob_attended = glob_out.astype(jnp.float32)
    glob_delta = jnp.sum(glob_grad.astype(jnp.float32) * glob_attended, axis=-1)
    glob_dot = jnp.einsum("ghd,thd->hgt", glob_grad, value3, preferred_element_type=jnp.float32)
    glob_dscore = (glob_probs * (glob_dot - jnp.transpose(glob_delta)[..., None])).astype(
        jnp.bfloat16
    )
    query_part = scale * jnp.einsum(
        "hgt,thd->ghd", glob_dscore, key3, preferred_element_type=jnp.float32
    )
    key_from_glob = scale * jnp.einsum(
        "hgt,ghd->thd", glob_dscore, glob_query, preferred_element_type=jnp.float32
    )
    value_from_glob = jnp.einsum(
        "hgt,ghd->thd", glob_weights, glob_grad, preferred_element_type=jnp.float32
    )
    summed = lax.psum((query_part, grad_wide), "seq")
    grad_query = grad_query.at[target].add(summed[0], mode="drop")
    pair_grad = pair_grad.at[target].add(summed[1], mode="drop")
    grad_key = pair_grad[..., :HD] + key_from_glob
    grad_value = pair_grad[..., HD:] + value_from_glob
    return (
        attended.reshape(tokens, heads * HD),
        grad_query.reshape(tokens, heads * HD).astype(jnp.bfloat16),
        grad_key.reshape(tokens, heads * HD).astype(jnp.bfloat16),
        grad_value.reshape(tokens, heads * HD).astype(jnp.bfloat16),
    )


BIG = 1e30
LIMIT = 63 * 1024 * 1024
NT = (((1,), (1,)), ((), ()))
TN = (((0,), (0,)), ((), ()))
NN = (((1,), (0,)), ((), ()))


def mm(left, right, dims):
    return lax.dot_general(left, right, dims, preferred_element_type=jnp.float32)


def head_kernel(
    n, tokens, q_hbm, k_hbm, v_hbm, g_hbm, rb_hbm, gp_hbm, att_ref, dq_ref, dk_ref, dv_ref,
    q_ref, k_ref, v_ref, g_ref, rb_ref, gp_ref, kq_send, v_send, g_send, tab_send, kq, vp, gp, tab,
    att_send, dv_send, dq_send, dk_send, att, dv, dq, dk,
    ka, qa, va, ga, probs, weights, dscore, load_sem, turn, send_sem, recv_sem,
):
    me = lax.axis_index("seq")
    total = n * tokens
    part = tokens // 2
    qb = tokens // BLK
    scale = 1.0 / math.sqrt(HD)
    half = me // 2
    inner = (me % 3 + 1) // 2
    near, far, mate = 2 - 2 * half, 3 - 2 * half, 1 - me + 4 * half
    others = [
        inner * mate + (1 - inner) * near,
        inner * near + (1 - inner) * far,
        inner * far + (1 - inner) * mate,
    ]

    barrier = pltpu.get_barrier_semaphore()
    for peer in others:
        pl.semaphore_signal(
            barrier, inc=1, device_id={"seq": peer}, device_id_type=pl.DeviceIdType.MESH
        )
    loads = [
        pltpu.make_async_copy(hbm, vmem, load_sem.at[i])
        for i, (hbm, vmem) in enumerate(
            ((k_hbm, k_ref), (q_hbm, q_ref), (v_hbm, v_ref), (g_hbm, g_ref), (rb_hbm, rb_ref), (gp_hbm, gp_ref))
        )
    ]
    for i in (4, 0, 1, 2, 3, 5):
        loads[i].start()

    stages = (
        (tab_send, tab), (kq_send, kq), (v_send, vp), (g_send, gp),
        (att_send, att), (dv_send, dv), (dq_send, dq), (dk_send, dk),
    )

    def copy(stage, peer, slot):
        send, recv = stages[stage]
        return pltpu.make_async_remote_copy(
            src_ref=send.at[peer],
            dst_ref=recv.at[slot],
            send_sem=send_sem.at[stage, peer],
            recv_sem=recv_sem.at[stage, slot],
            device_id={"seq": peer},
            device_id_type=pl.DeviceIdType.MESH,
        )

    def start(stage, peer):
        copy(stage, peer, me).start()

    def arrive(stage):
        for peer in others:
            copy(stage, peer, peer).wait_recv()

    def keep(stage):
        send, recv = stages[stage]
        recv[me] = send[me]

    def fold(ref, slot, rows):
        ref[slot, :, 0:HD] = rows[0:part]
        ref[slot, :, HD : 2 * HD] = rows[part:tokens]

    def fold_t(ref, slot, columns):
        stacked = jnp.concatenate([columns[:, 0:part], columns[:, part:tokens]], axis=0)
        ref[slot] = stacked.T.astype(jnp.bfloat16)

    lane = lax.broadcasted_iota(jnp.int32, (1, 128), 1)
    loads[4].wait()
    for h in range(n):
        mark = jnp.zeros((1, 128), jnp.int32)
        for r in range(RAND):
            for b in range(qb):
                at = lax.rem(HD + r * 8 * n + 8 * me + b, 128)
                mark = jnp.where(lane == at, rb_ref[r, h, b], mark)
        tab_send[h] = mark
    loads[0].wait()
    loads[1].wait()
    for h in range(n):
        cols = slice(h * HD, (h + 1) * HD)
        kq_send[h, :, 0:HD] = k_ref[:, cols]
        kq_send[h, :, HD : 2 * HD] = q_ref[:, cols] * jnp.bfloat16(scale)
    pl.semaphore_wait(barrier, n - 1)
    for peer in others:
        start(0, peer)
        start(1, peer)
    loads[2].wait()
    for h in range(n):
        fold(v_send, h, v_ref[:, h * HD : (h + 1) * HD])
    loads[3].wait()
    for h in range(n):
        fold(g_send, h, g_ref[:, h * HD : (h + 1) * HD])

    def take_turns(stage):
        copy(stage, near, me).wait_send()

        @pl.when(inner == 1)
        def _():
            pl.semaphore_signal(
                turn.at[stage - 1], inc=1, device_id={"seq": mate}, device_id_type=pl.DeviceIdType.MESH
            )

        @pl.when(inner == 0)
        def _():
            pl.semaphore_wait(turn.at[stage - 1], 1)

        for peer in others:
            start(stage + 1, peer)

    pos = lax.broadcasted_iota(jnp.int32, (total, 128), 0)
    col = lax.broadcasted_iota(jnp.int32, (total, 128), 1)
    loads[5].wait()
    globals_here = gp_ref.shape[1]
    spots = lax.broadcasted_iota(jnp.int32, (total, globals_here), 0) == gp_ref[...]
    spread = mm(
        jnp.where(spots, 1.0, 0.0).astype(jnp.bfloat16),
        jnp.ones((globals_here, 128), jnp.bfloat16),
        NN,
    )
    is_global = spread > 0.5
    slot = col - HD
    block = (slot // 8) * qb + slot % 8
    mine = (slot >= 0) & (slot < 8 * n) & (slot % 8 < qb)
    key_block = pos // BLK
    window = mine & (block - key_block <= 1) & (key_block - block <= 1)
    open_key = window | is_global
    hot = jnp.where(mine & (block == key_block) & jnp.logical_not(is_global), 1.0, 0.0)

    take_turns(1)
    for stage in range(4):
        keep(stage)

    arrive(0)
    picks = tab[0]
    for c in range(1, n):
        picks = picks + tab[c]
    for r in range(RAND):
        shifted = picks if r == 0 else pltpu.roll(picks, 128 - r * 8 * n, 1)
        open_key = open_key | (mine & (key_block == shifted))
    bias = jnp.where(open_key, 0.0, -BIG).astype(jnp.bfloat16)
    arrive(1)
    pair = kq[...].reshape(total, 128)
    ka[...] = bias
    ka[:, 0:HD] = pair[:, 0:HD]
    qa[...] = hot.astype(jnp.bfloat16)
    qa[:, 0:HD] = pair[:, HD : 2 * HD]

    keys = ka[...]
    for a in range(n):
        score = mm(keys, qa[a * tokens : (a + 1) * tokens, :], NT)
        top = jnp.max(score, axis=0, keepdims=True)
        raised = jnp.exp(score - top)
        prob = raised * (1.0 / jnp.sum(raised, axis=0, keepdims=True))
        probs[a] = prob
        weights[a] = prob.astype(jnp.bfloat16)
    keys_t = keys[:, 0:HD].T
    take_turns(2)

    order = others + [me]
    arrive(2)
    for c in range(n):
        va[c * tokens : c * tokens + part, :] = vp[c, :, 0:HD]
        va[c * tokens + part : (c + 1) * tokens, :] = vp[c, :, HD : 2 * HD]
    values = va[...]
    values_t = values.T
    outs = []
    for a in order:
        out = mm(values_t, weights[a], NN)
        fold_t(att_send, a, out)
        if a is not me:
            start(4, a)
        outs.append(out.astype(jnp.bfloat16).astype(jnp.float32))

    arrive(3)
    for c in range(n):
        ga[c, 0:part, :] = gp[c, :, 0:HD]
        ga[c, part:tokens, :] = gp[c, :, HD : 2 * HD]

    def value_grad(a):
        rows = pl.ds(pl.multiple_of(a * tokens, tokens), tokens)
        grad = jnp.zeros((tokens, HD), jnp.float32)
        for c in range(n):
            grad = grad + mm(weights[c, rows, :], ga[c], NN)
        fold(dv_send, a, grad.astype(jnp.bfloat16))

    def score_grad(a, out):
        grad = ga[a]
        delta = jnp.sum(grad.astype(jnp.float32).T * out, axis=0, keepdims=True)
        dprob = mm(values, grad, NT)
        dscore[a] = (probs[a] * (dprob - delta)).astype(jnp.bfloat16)

    def query_grad(a):
        fold_t(dq_send, a, mm(keys_t, dscore[a], NN) * scale)

    def key_grad(a):
        rows = pl.ds(pl.multiple_of(a * tokens, tokens), tokens)
        grad = jnp.zeros((tokens, HD), jnp.float32)
        for c in range(n):
            grad = grad + mm(dscore[c, rows, :], qa[c * tokens : (c + 1) * tokens, 0:HD], NN)
        fold(dk_send, a, grad.astype(jnp.bfloat16))

    value_grad(order[0])
    start(5, order[0])
    value_grad(order[1])
    start(5, order[1])
    value_grad(order[2])
    start(5, order[2])
    score_grad(order[0], outs[0])
    query_grad(order[0])
    start(6, order[0])
    score_grad(order[1], outs[1])
    score_grad(order[2], outs[2])
    score_grad(order[3], outs[3])
    key_grad(order[0])
    start(7, order[0])
    query_grad(order[1])
    start(6, order[1])
    key_grad(order[1])
    start(7, order[1])
    query_grad(order[2])
    start(6, order[2])
    key_grad(order[2])
    start(7, order[2])
    value_grad(order[3])
    query_grad(order[3])
    key_grad(order[3])
    for stage in range(4, 8):
        keep(stage)

    for stage, ref in ((4, att_ref), (5, dv_ref), (6, dq_ref), (7, dk_ref)):
        arrive(stage)
        recv = stages[stage][1]
        for h in range(n):
            cols = slice(h * HD, (h + 1) * HD)
            ref[0:part, cols] = recv[h, :, 0:HD]
            ref[part:tokens, cols] = recv[h, :, HD : 2 * HD]
    for stage in range(len(stages)):
        for peer in (far, mate) if stage in (1, 2) else others:
            copy(stage, peer, me).wait_send()


def write_out(*refs):
    count = len(refs) // 2
    sources, targets, sem = refs[:count], refs[count : 2 * count], refs[-1]
    stores = [pltpu.make_async_copy(sources[i], targets[i], sem.at[i]) for i in range(count)]
    for store in stores:
        store.start()
    for store in stores:
        store.wait()


def local_heads(query_rows, key_rows, value_rows, out_grad, random_blocks, global_positions):
    tokens, width = query_rows.shape
    n = lax.axis_size("seq")
    total = n * tokens
    bf16, f32 = jnp.bfloat16, jnp.float32
    where_it_lies = pl.BlockSpec(memory_space=pltpu.HBM)
    rows = [pltpu.VMEM((tokens, width), bf16)] * 4
    whole = pltpu.VMEM((n, tokens, 2 * HD), bf16)
    folded = pltpu.VMEM((n, tokens // 2, 2 * HD), bf16)
    small = pltpu.VMEM((n, 1, 128), jnp.int32)
    results = pl.pallas_call(
        partial(head_kernel, n, tokens),
        out_shape=[pltpu.VMEM((tokens, width), bf16)] * 4,
        in_specs=[where_it_lies] * 6,
        out_specs=[pl.BlockSpec(memory_space=pltpu.VMEM)] * 4,
        scratch_shapes=[
            *rows,
            pltpu.SMEM((RAND,) + random_blocks.shape[:2], jnp.int32),
            pltpu.VMEM((1, global_positions.shape[0]), jnp.int32),
            whole, folded, folded, small,
            whole, folded, folded, small,
            *([folded] * 8),
            pltpu.VMEM((total, 128), bf16),
            pltpu.VMEM((total, 128), bf16),
            pltpu.VMEM((total, HD), bf16),
            pltpu.VMEM((n, tokens, HD), bf16),
            pltpu.VMEM((n, total, tokens), f32),
            pltpu.VMEM((n, total, tokens), bf16),
            pltpu.VMEM((n, total, tokens), bf16),
            pltpu.SemaphoreType.DMA((6,)),
            pltpu.SemaphoreType.REGULAR((2,)),
            pltpu.SemaphoreType.DMA((8, n)),
            pltpu.SemaphoreType.DMA((8, n)),
        ],
        compiler_params=pltpu.CompilerParams(
            collective_id=0, has_side_effects=True, vmem_limit_bytes=LIMIT
        ),
        cost_estimate=pl.CostEstimate(
            flops=14 * total * total * HD, bytes_accessed=16 * tokens * width, transcendentals=total * total
        ),
    )(
        query_rows, key_rows, value_rows, out_grad,
        jnp.transpose(random_blocks, (2, 0, 1)), global_positions.reshape(1, -1),
    )
    return pl.pallas_call(
        write_out,
        out_shape=[jax.ShapeDtypeStruct((tokens, width), bf16)] * 4,
        in_specs=[pl.BlockSpec(memory_space=pltpu.VMEM)] * 4,
        out_specs=[where_it_lies] * 4,
        scratch_shapes=[pltpu.SemaphoreType.DMA((4,))],
    )(*(pltpu.with_memory_space_constraint(r, pltpu.VMEM) for r in results))


def local(query_rows, key_rows, value_rows, out_grad, random_blocks, global_positions):
    n = lax.axis_size("seq")
    tokens = query_rows.shape[0]
    one_head_each = query_rows.shape[1] == n * HD and n > 1
    fits = n == 4 and 8 * n <= 128 - HD and tokens // BLK <= 8 and n * tokens // BLK <= 128
    if one_head_each and fits and tokens % 256 == 0 and n * tokens <= 1024:
        run = local_heads
    else:
        run = local_wide
    return run(query_rows, key_rows, value_rows, out_grad, random_blocks, global_positions)


def solution(mesh):
    placed = (
        P(("groups", "seq"), ("head", "pair")),
        P(("groups", "seq"), ("head", "pair")),
        P(("groups", "seq"), ("head", "pair")),
        P(("groups", "seq"), ("head", "pair")),
        P(("groups", "head", "pair"), "seq", None),
        P("groups"),
    )
    return jax.shard_map(
        local,
        mesh=mesh,
        in_specs=placed,
        out_specs=(
            P(("groups", "seq"), ("head", "pair")),
            P(("groups", "seq"), ("head", "pair")),
            P(("groups", "seq"), ("head", "pair")),
            P(("groups", "seq"), ("head", "pair")),
        ),
        check_vma=False,
    )
```

```python
from functools import partial
import math

import jax
import jax.numpy as jnp
from jax import lax
from jax.experimental import pallas as pl
from jax.experimental.pallas import tpu as pltpu
from jax.sharding import PartitionSpec as P

HD = 64
BLK = 64
RAND = 3


def padded_2(array, sides, width):
    for axis, dim in sides:
        peers, length = (lax.axis_size(axis), array.shape[dim])
        up = [(i, (i + 1) % peers) for i in range(peers - 1)]
        down = [(j, i) for i, j in up]
        last = lax.slice_in_dim(array, length - width, length, axis=dim)
        leading = lax.slice_in_dim(array, 0, width, axis=dim)
        before = lax.ppermute(last, axis, up)
        after = lax.ppermute(leading, axis, down)
        array = jnp.concatenate([before, array, after], axis=dim)
    return array


def from_behind(array, axis, by):
    peers = lax.axis_size(axis)
    pairs = [(i, i + by) for i in range(peers) if 0 <= i + by < peers]
    return lax.ppermute(array, axis, pairs)


def softmax_rows(scores):
    top = jnp.max(scores, axis=-1, keepdims=True)
    raised = jnp.exp(scores - top)
    return raised / jnp.sum(raised, axis=-1, keepdims=True)


def group_probs(query, window, far_rows, global_rows, window_valid, global_keep, scale):
    near = (
        jnp.einsum("bihd,bjhd->bhij", query, window[..., :HD], preferred_element_type=jnp.float32)
        * scale
    )
    far = (
        jnp.einsum("bihd,bjhd->bhij", query, far_rows[..., :HD], preferred_element_type=jnp.float32)
        * scale
    )
    wide = (
        jnp.einsum(
            "bihd,jhd->bhij", query, global_rows[..., :HD], preferred_element_type=jnp.float32
        )
        * scale
    )
    near = jnp.where(window_valid[:, None, None, :], near, -jnp.inf)
    wide = jnp.where(global_keep[:, :, None, :], wide, -jnp.inf)
    return softmax_rows(jnp.concatenate([near, far, wide], axis=-1))


def split_keys(values, window, far_rows):
    span = window.shape[1]
    reach = far_rows.shape[1]
    return (values[..., :span], values[..., span : span + reach], values[..., span + reach :])


def forward_group(items, global_rows, scale):
    query, window, far_rows, window_valid, global_keep = items
    weights = group_probs(
        query, window, far_rows, global_rows, window_valid, global_keep, scale
    ).astype(jnp.bfloat16)
    near, far, wide = split_keys(weights, window, far_rows)
    out = jnp.einsum("bhij,bjhd->bihd", near, window[..., HD:], preferred_element_type=jnp.float32)
    out = out + jnp.einsum(
        "bhij,bjhd->bihd", far, far_rows[..., HD:], preferred_element_type=jnp.float32
    )
    return out + jnp.einsum(
        "bhij,jhd->bihd", wide, global_rows[..., HD:], preferred_element_type=jnp.float32
    )


def backward_group(items, global_rows, scale):
    query, window, far_rows, window_valid, global_keep, grad_out, delta = items
    probs = group_probs(query, window, far_rows, global_rows, window_valid, global_keep, scale)
    weights = probs.astype(jnp.bfloat16)
    value_dot = jnp.concatenate(
        [
            jnp.einsum(
                "bihd,bjhd->bhij", grad_out, window[..., HD:], preferred_element_type=jnp.float32
            ),
            jnp.einsum(
                "bihd,bjhd->bhij", grad_out, far_rows[..., HD:], preferred_element_type=jnp.float32
            ),
            jnp.einsum(
                "bihd,jhd->bhij",
                grad_out,
                global_rows[..., HD:],
                preferred_element_type=jnp.float32,
            ),
        ],
        axis=-1,
    )
    dscore = (probs * (value_dot - jnp.transpose(delta, (0, 2, 1))[..., None])).astype(jnp.bfloat16)
    dnear, dfar, dwide = split_keys(dscore, window, far_rows)
    near, far, wide = split_keys(weights, window, far_rows)
    grad_query = jnp.einsum(
        "bhij,bjhd->bihd", dnear, window[..., :HD], preferred_element_type=jnp.float32
    )
    grad_query = grad_query + jnp.einsum(
        "bhij,bjhd->bihd", dfar, far_rows[..., :HD], preferred_element_type=jnp.float32
    )
    grad_query = scale * (
        grad_query
        + jnp.einsum(
            "bhij,jhd->bihd", dwide, global_rows[..., :HD], preferred_element_type=jnp.float32
        )
    )
    grad_window = jnp.concatenate(
        [
            scale * jnp.einsum("bhij,bihd->bjhd", dnear, query, preferred_element_type=jnp.float32),
            jnp.einsum("bhij,bihd->bjhd", near, grad_out, preferred_element_type=jnp.float32),
        ],
        axis=-1,
    )
    grad_far = jnp.concatenate(
        [
            scale * jnp.einsum("bhij,bihd->bjhd", dfar, query, preferred_element_type=jnp.float32),
            jnp.einsum("bhij,bihd->bjhd", far, grad_out, preferred_element_type=jnp.float32),
        ],
        axis=-1,
    ).astype(jnp.bfloat16)
    grad_wide = jnp.concatenate(
        [
            scale * jnp.einsum("bhij,bihd->jhd", dwide, query, preferred_element_type=jnp.float32),
            jnp.einsum("bhij,bihd->jhd", wide, grad_out, preferred_element_type=jnp.float32),
        ],
        axis=-1,
    )
    return (grad_query, grad_window, grad_far, grad_wide)


def local_wide(query_rows, key_rows, value_rows, out_grad, random_blocks, global_positions):
    tokens = query_rows.shape[0]
    heads = query_rows.shape[1] // HD
    blocks = tokens // BLK
    devices = lax.axis_size("seq")
    place = lax.axis_index("seq")
    scale = 1.0 / math.sqrt(HD)
    capacity = RAND * (blocks // (devices - 1)) + min(RAND, blocks % (devices - 1))
    group = math.gcd(blocks, max(1, 512 // BLK))
    count = blocks // group
    local_index = global_positions - place * tokens
    owned = (local_index >= 0) & (local_index < tokens)
    target = jnp.where(owned, local_index, tokens)
    safe_index = jnp.where(owned, local_index, 0)

    def pick(rows):
        return jnp.where(owned[:, None], rows[safe_index].astype(jnp.float32), 0.0)

    glob_sum = (
        lax.psum(pick(query_rows).astype(jnp.bfloat16), "seq").astype(jnp.float32),
        lax.psum(pick(key_rows).astype(jnp.bfloat16), "seq").astype(jnp.float32),
        lax.psum(pick(value_rows).astype(jnp.bfloat16), "seq").astype(jnp.float32),
        lax.psum(pick(out_grad).astype(jnp.bfloat16), "seq").astype(jnp.float32),
    )
    glob_query = glob_sum[0].astype(jnp.bfloat16).reshape(-1, heads, HD)
    glob_key = glob_sum[1].astype(jnp.bfloat16).reshape(-1, heads, HD)
    glob_value = glob_sum[2].astype(jnp.bfloat16).reshape(-1, heads, HD)
    glob_grad = glob_sum[3].astype(jnp.bfloat16).reshape(-1, heads, HD)
    global_rows = jnp.concatenate([glob_key, glob_value], axis=-1)
    query3 = query_rows.reshape(tokens, heads, HD)
    key3 = key_rows.reshape(tokens, heads, HD)
    value3 = value_rows.reshape(tokens, heads, HD)
    pair_rows = jnp.concatenate([key3, value3], axis=-1)
    padded = padded_2(pair_rows, (("seq", 0),), BLK)
    framed = padded.reshape(blocks + 2, BLK, heads, 2 * HD)
    window = jnp.concatenate([framed[:-2], framed[1:-1], framed[2:]], axis=1)
    block_ids = place * blocks + jnp.arange(blocks)
    neighbour = block_ids[:, None] + (jnp.repeat(jnp.arange(3), BLK) - 1)[None, :]
    window_valid = (neighbour >= 0) & (neighbour < devices * blocks)
    global_block = global_positions // BLK
    near_glob = jnp.abs(global_block[None, :] - block_ids[:, None]) <= 1
    in_random = jnp.any(random_blocks[:, :, :, None] == global_block[None, None, None, :], axis=2)
    global_keep = jnp.logical_not(near_glob[:, None, :] | jnp.transpose(in_random, (1, 0, 2)))
    owner = random_blocks // blocks
    local_block = random_blocks % blocks
    flat_owner = owner.reshape(heads, blocks * RAND)
    hits = (flat_owner[:, :, None] == jnp.arange(devices)[None, None, :]).astype(jnp.int32)
    before = jnp.cumsum(hits, axis=1) - hits
    flat_slot = jnp.sum(before * hits, axis=2)
    placed = (flat_slot[:, :, None] == jnp.arange(capacity)[None, None, :]).astype(jnp.int32)
    marks = (local_block.reshape(heads, blocks * RAND) + 1)[:, :, None, None]
    table = jnp.sum(hits[:, :, :, None] * placed[:, :, None, :] * marks, axis=1) - 1
    asked = lax.all_to_all(
        jnp.transpose(table, (1, 0, 2)), "seq", split_axis=0, concat_axis=0, tiled=True
    )
    own_blocks = pair_rows.reshape(blocks, BLK, heads, 2 * HD)
    wanted = (jnp.maximum(asked, 0)[..., None] == jnp.arange(blocks)).astype(jnp.bfloat16)
    served = jnp.einsum(
        "zhcb,bthf->zhctf", wanted, own_blocks, preferred_element_type=jnp.float32
    ).astype(jnp.bfloat16)
    owner_order = jnp.transpose(owner, (1, 2, 0))
    slot_order = jnp.transpose(flat_slot.reshape(heads, blocks, RAND), (1, 2, 0))
    head_order = jnp.arange(heads)[None, None, :]
    arrived = lax.all_to_all(served, "seq", split_axis=0, concat_axis=0, tiled=True)
    arrived = jnp.transpose(arrived, (0, 2, 1, 3, 4)).reshape(
        devices * capacity, heads, BLK, 2 * HD
    )
    source = owner_order * capacity + slot_order
    chosen = (source[..., None] == jnp.arange(devices * capacity)).astype(jnp.bfloat16)
    picked = jnp.einsum(
        "brhz,zhtf->brhtf", chosen, arrived, preferred_element_type=jnp.float32
    ).astype(jnp.bfloat16)
    far_rows = jnp.transpose(picked, (0, 1, 3, 2, 4)).reshape(blocks, RAND * BLK, heads, 2 * HD)

    def grouped(array):
        return array.reshape((count, group) + array.shape[1:])

    query_blocks = query3.reshape(blocks, BLK, heads, HD)
    sparse_out = lax.map(
        partial(forward_group, global_rows=global_rows, scale=scale),
        (
            grouped(query_blocks),
            grouped(window),
            grouped(far_rows),
            grouped(window_valid),
            grouped(global_keep),
        ),
    )
    sparse_out = sparse_out.reshape(tokens, heads, HD)
    wide = jnp.einsum("ghd,thd->hgt", glob_query, key3, preferred_element_type=jnp.float32) * scale
    local_top = jnp.max(wide, axis=-1)
    top = lax.pmax(local_top, "seq")
    total = lax.psum(jnp.sum(jnp.exp(wide - top[..., None]), axis=-1), "seq")
    glob_probs = jnp.exp(wide - top[..., None]) / total[..., None]
    glob_weights = glob_probs.astype(jnp.bfloat16)
    glob_part = jnp.einsum("hgt,thd->ghd", glob_weights, value3, preferred_element_type=jnp.float32)
    glob_out = lax.psum(glob_part, "seq").astype(jnp.bfloat16)
    attended = sparse_out.astype(jnp.bfloat16).at[target].set(glob_out, mode="drop")
    glob_mask = jnp.zeros((tokens,), jnp.bool_).at[target].set(True, mode="drop")
    sparse_grad = jnp.where(
        glob_mask[:, None, None],
        jnp.zeros_like(out_grad.reshape(tokens, heads, HD)),
        out_grad.reshape(tokens, heads, HD),
    )
    delta = jnp.sum(sparse_grad.astype(jnp.float32) * attended.astype(jnp.float32), axis=-1)
    grad_query, grad_window, grad_far, grad_wide = lax.map(
        partial(backward_group, global_rows=global_rows, scale=scale),
        (
            grouped(query_blocks),
            grouped(window),
            grouped(far_rows),
            grouped(window_valid),
            grouped(global_keep),
            grouped(sparse_grad.reshape(blocks, BLK, heads, HD)),
            grouped(delta.reshape(blocks, BLK, heads)),
        ),
    )
    grad_query = grad_query.reshape(tokens, heads, HD)
    grad_window = grad_window.reshape(blocks, 3, BLK, heads, 2 * HD)
    grad_wide = jnp.sum(grad_wide, axis=0)
    folded = jnp.zeros((blocks + 2, BLK, heads, 2 * HD), jnp.float32)
    folded = (
        folded.at[0:blocks]
        .add(grad_window[:, 0])
        .at[1 : blocks + 1]
        .add(grad_window[:, 1])
        .at[2 : blocks + 2]
        .add(grad_window[:, 2])
    )
    from_right = from_behind(folded[0], "seq", -1)
    from_left = from_behind(folded[blocks + 1], "seq", 1)
    local_pair = folded[1 : blocks + 1]
    local_pair = local_pair.at[blocks - 1].add(from_right).at[0].add(from_left)
    far_terms = jnp.transpose(grad_far.reshape(blocks, RAND, BLK, heads, 2 * HD), (0, 1, 3, 2, 4))
    outgoing = (
        jnp.zeros((devices, heads, capacity, BLK, 2 * HD), jnp.bfloat16)
        .at[owner_order, head_order, slot_order]
        .set(far_terms)
    )
    returned = lax.all_to_all(outgoing, "seq", split_axis=0, concat_axis=0, tiled=True)
    landing = jnp.where(asked >= 0, asked, blocks)
    gathered = (
        jnp.zeros((blocks, heads, BLK, 2 * HD), jnp.float32)
        .at[landing, jnp.arange(heads)[None, :, None]]
        .add(returned.astype(jnp.float32), mode="drop")
    )
    pair_grad = local_pair.reshape(tokens, heads, 2 * HD) + jnp.transpose(
        gathered, (0, 2, 1, 3)
    ).reshape(tokens, heads, 2 * HD)
    glob_attended = glob_out.astype(jnp.float32)
    glob_delta = jnp.sum(glob_grad.astype(jnp.float32) * glob_attended, axis=-1)
    glob_dot = jnp.einsum("ghd,thd->hgt", glob_grad, value3, preferred_element_type=jnp.float32)
    glob_dscore = (glob_probs * (glob_dot - jnp.transpose(glob_delta)[..., None])).astype(
        jnp.bfloat16
    )
    query_part = scale * jnp.einsum(
        "hgt,thd->ghd", glob_dscore, key3, preferred_element_type=jnp.float32
    )
    key_from_glob = scale * jnp.einsum(
        "hgt,ghd->thd", glob_dscore, glob_query, preferred_element_type=jnp.float32
    )
    value_from_glob = jnp.einsum(
        "hgt,ghd->thd", glob_weights, glob_grad, preferred_element_type=jnp.float32
    )
    summed = lax.psum((query_part, grad_wide), "seq")
    grad_query = grad_query.at[target].add(summed[0], mode="drop")
    pair_grad = pair_grad.at[target].add(summed[1], mode="drop")
    grad_key = pair_grad[..., :HD] + key_from_glob
    grad_value = pair_grad[..., HD:] + value_from_glob
    return (
        attended.reshape(tokens, heads * HD),
        grad_query.reshape(tokens, heads * HD).astype(jnp.bfloat16),
        grad_key.reshape(tokens, heads * HD).astype(jnp.bfloat16),
        grad_value.reshape(tokens, heads * HD).astype(jnp.bfloat16),
    )


BIG = 1e30
LIMIT = 63 * 1024 * 1024
NT = (((1,), (1,)), ((), ()))
TN = (((0,), (0,)), ((), ()))
NN = (((1,), (0,)), ((), ()))


def mm(left, right, dims):
    return lax.dot_general(left, right, dims, preferred_element_type=jnp.float32)


def head_kernel(
    n, tokens, q_hbm, k_hbm, v_hbm, g_hbm, rb_hbm, gp_hbm, att_ref, dq_ref, dk_ref, dv_ref,
    q_ref, k_ref, v_ref, g_ref, rb_ref, gp_ref, kq_send, v_send, g_send, tab_send, kq, vp, gp, tab,
    att_send, dv_send, dq_send, dk_send, att, dv, dq, dk,
    ka, qa, va, ga, probs, weights, dscore, load_sem, turn, send_sem, recv_sem,
):
    me = lax.axis_index("seq")
    total = n * tokens
    part = tokens // 2
    qb = tokens // BLK
    scale = 1.0 / math.sqrt(HD)
    half = me // 2
    inner = (me % 3 + 1) // 2
    near, far, mate = 2 - 2 * half, 3 - 2 * half, 1 - me + 4 * half
    others = [
        inner * mate + (1 - inner) * near,
        inner * near + (1 - inner) * far,
        inner * far + (1 - inner) * mate,
    ]

    barrier = pltpu.get_barrier_semaphore()
    for peer in others:
        pl.semaphore_signal(
            barrier, inc=1, device_id={"seq": peer}, device_id_type=pl.DeviceIdType.MESH
        )
    loads = [
        pltpu.make_async_copy(hbm, vmem, load_sem.at[i])
        for i, (hbm, vmem) in enumerate(
            ((k_hbm, k_ref), (q_hbm, q_ref), (v_hbm, v_ref), (g_hbm, g_ref), (rb_hbm, rb_ref), (gp_hbm, gp_ref))
        )
    ]
    for i in (4, 0, 1, 2, 3, 5):
        loads[i].start()

    stages = (
        (tab_send, tab), (kq_send, kq), (v_send, vp), (g_send, gp),
        (att_send, att), (dv_send, dv), (dq_send, dq), (dk_send, dk),
    )

    def copy(stage, peer, slot):
        send, recv = stages[stage]
        return pltpu.make_async_remote_copy(
            src_ref=send.at[peer],
            dst_ref=recv.at[slot],
            send_sem=send_sem.at[stage, peer],
            recv_sem=recv_sem.at[stage, slot],
            device_id={"seq": peer},
            device_id_type=pl.DeviceIdType.MESH,
        )

    def start(stage, peer):
        copy(stage, peer, me).start()

    def arrive(stage):
        for peer in others:
            copy(stage, peer, peer).wait_recv()

    def keep(stage):
        send, recv = stages[stage]
        recv[me] = send[me]

    def fold(ref, slot, rows):
        ref[slot, :, 0:HD] = rows[0:part]
        ref[slot, :, HD : 2 * HD] = rows[part:tokens]

    def fold_t(ref, slot, columns):
        stacked = jnp.concatenate([columns[:, 0:part], columns[:, part:tokens]], axis=0)
        ref[slot] = stacked.T.astype(jnp.bfloat16)

    lane = lax.broadcasted_iota(jnp.int32, (1, 128), 1)
    loads[4].wait()
    for h in range(n):
        mark = jnp.zeros((1, 128), jnp.int32)
        for r in range(RAND):
            for b in range(qb):
                at = lax.rem(HD + r * 8 * n + 8 * me + b, 128)
                mark = jnp.where(lane == at, rb_ref[r, h, b], mark)
        tab_send[h] = mark
    loads[0].wait()
    loads[1].wait()
    for h in range(n):
        cols = slice(h * HD, (h + 1) * HD)
        kq_send[h, :, 0:HD] = k_ref[:, cols]
        kq_send[h, :, HD : 2 * HD] = q_ref[:, cols] * jnp.bfloat16(scale)
    pl.semaphore_wait(barrier, n - 1)
    @pl.when(inner == 1)
    def _():
        for peer in others:
            start(0, peer)
            start(1, peer)

    loads[2].wait()
    for h in range(n):
        fold(v_send, h, v_ref[:, h * HD : (h + 1) * HD])
    loads[3].wait()
    for h in range(n):
        fold(g_send, h, g_ref[:, h * HD : (h + 1) * HD])

    @pl.when(inner == 1)
    def _():
        for stage in (2, 3):
            for peer in others:
                start(stage, peer)
        copy(1, mate, me).wait_send()
        pl.semaphore_signal(turn, inc=1, device_id={"seq": mate}, device_id_type=pl.DeviceIdType.MESH)

    pos = lax.broadcasted_iota(jnp.int32, (total, 128), 0)
    col = lax.broadcasted_iota(jnp.int32, (total, 128), 1)
    loads[5].wait()
    globals_here = gp_ref.shape[1]
    spots = lax.broadcasted_iota(jnp.int32, (total, globals_here), 0) == gp_ref[...]
    spread = mm(
        jnp.where(spots, 1.0, 0.0).astype(jnp.bfloat16),
        jnp.ones((globals_here, 128), jnp.bfloat16),
        NN,
    )
    is_global = spread > 0.5
    slot = col - HD
    block = (slot // 8) * qb + slot % 8
    mine = (slot >= 0) & (slot < 8 * n) & (slot % 8 < qb)
    key_block = pos // BLK
    window = mine & (block - key_block <= 1) & (key_block - block <= 1)
    open_key = window | is_global
    hot = jnp.where(mine & (block == key_block) & jnp.logical_not(is_global), 1.0, 0.0)

    @pl.when(inner == 0)
    def _():
        pl.semaphore_wait(turn, 1)
        for stage in (0, 1, 2):
            for peer in others:
                start(stage, peer)

    for stage in range(4):
        keep(stage)

    @pl.when(inner == 0)
    def _():
        copy(2, far, me).wait_send()
        for peer in others:
            start(3, peer)

    arrive(0)
    picks = tab[0]
    for c in range(1, n):
        picks = picks + tab[c]
    for r in range(RAND):
        shifted = picks if r == 0 else pltpu.roll(picks, 128 - r * 8 * n, 1)
        open_key = open_key | (mine & (key_block == shifted))
    bias = jnp.where(open_key, 0.0, -BIG).astype(jnp.bfloat16)
    arrive(1)
    pair = kq[...].reshape(total, 128)
    ka[...] = bias
    ka[:, 0:HD] = pair[:, 0:HD]
    qa[...] = hot.astype(jnp.bfloat16)
    qa[:, 0:HD] = pair[:, HD : 2 * HD]

    keys = ka[...]
    for a in range(n):
        score = mm(keys, qa[a * tokens : (a + 1) * tokens, :], NT)
        top = jnp.max(score, axis=0, keepdims=True)
        raised = jnp.exp(score - top)
        prob = raised * (1.0 / jnp.sum(raised, axis=0, keepdims=True))
        probs[a] = prob
        weights[a] = prob.astype(jnp.bfloat16)
    keys_t = keys[:, 0:HD].T

    order = others + [me]
    arrive(2)
    for c in range(n):
        va[c * tokens : c * tokens + part, :] = vp[c, :, 0:HD]
        va[c * tokens + part : (c + 1) * tokens, :] = vp[c, :, HD : 2 * HD]
    values = va[...]
    values_t = values.T
    outs = []
    for a in order:
        out = mm(values_t, weights[a], NN)
        fold_t(att_send, a, out)
        if a is not me:
            start(4, a)
        outs.append(out.astype(jnp.bfloat16).astype(jnp.float32))

    arrive(3)
    for c in range(n):
        ga[c, 0:part, :] = gp[c, :, 0:HD]
        ga[c, part:tokens, :] = gp[c, :, HD : 2 * HD]

    def value_grad(a):
        rows = pl.ds(pl.multiple_of(a * tokens, tokens), tokens)
        grad = jnp.zeros((tokens, HD), jnp.float32)
        for c in range(n):
            grad = grad + mm(weights[c, rows, :], ga[c], NN)
        fold(dv_send, a, grad.astype(jnp.bfloat16))

    def score_grad(a, out):
        grad = ga[a]
        delta = jnp.sum(grad.astype(jnp.float32).T * out, axis=0, keepdims=True)
        dprob = mm(values, grad, NT)
        dscore[a] = (probs[a] * (dprob - delta)).astype(jnp.bfloat16)

    def query_grad(a):
        fold_t(dq_send, a, mm(keys_t, dscore[a], NN) * scale)

    def key_grad(a):
        rows = pl.ds(pl.multiple_of(a * tokens, tokens), tokens)
        grad = jnp.zeros((tokens, HD), jnp.float32)
        for c in range(n):
            grad = grad + mm(dscore[c, rows, :], qa[c * tokens : (c + 1) * tokens, 0:HD], NN)
        fold(dk_send, a, grad.astype(jnp.bfloat16))

    value_grad(order[0])
    start(5, order[0])
    value_grad(order[1])
    start(5, order[1])
    score_grad(order[0], outs[0])
    query_grad(order[0])
    start(6, order[0])
    score_grad(order[1], outs[1])
    score_grad(order[2], outs[2])
    score_grad(order[3], outs[3])
    key_grad(order[0])
    start(7, order[0])
    query_grad(order[1])
    start(6, order[1])
    key_grad(order[1])
    start(7, order[1])
    value_grad(order[2])
    start(5, order[2])
    query_grad(order[2])
    start(6, order[2])
    key_grad(order[2])
    start(7, order[2])
    value_grad(order[3])
    query_grad(order[3])
    key_grad(order[3])
    for stage in range(4, 8):
        keep(stage)

    for stage, ref in ((4, att_ref), (5, dv_ref), (6, dq_ref), (7, dk_ref)):
        arrive(stage)
        recv = stages[stage][1]
        for h in range(n):
            cols = slice(h * HD, (h + 1) * HD)
            ref[0:part, cols] = recv[h, :, 0:HD]
            ref[part:tokens, cols] = recv[h, :, HD : 2 * HD]
    @pl.when(inner == 1)
    def _():
        copy(2, far, me).wait_send()

    @pl.when(inner == 0)
    def _():
        copy(1, mate, me).wait_send()

    for stage in range(len(stages)):
        for peer in (near, far) if stage == 1 else (mate, near) if stage == 2 else others:
            copy(stage, peer, me).wait_send()


def write_out(*refs):
    count = len(refs) // 2
    sources, targets, sem = refs[:count], refs[count : 2 * count], refs[-1]
    stores = [pltpu.make_async_copy(sources[i], targets[i], sem.at[i]) for i in range(count)]
    for store in stores:
        store.start()
    for store in stores:
        store.wait()


def local_heads(query_rows, key_rows, value_rows, out_grad, random_blocks, global_positions):
    tokens, width = query_rows.shape
    n = lax.axis_size("seq")
    total = n * tokens
    bf16, f32 = jnp.bfloat16, jnp.float32
    where_it_lies = pl.BlockSpec(memory_space=pltpu.HBM)
    rows = [pltpu.VMEM((tokens, width), bf16)] * 4
    whole = pltpu.VMEM((n, tokens, 2 * HD), bf16)
    folded = pltpu.VMEM((n, tokens // 2, 2 * HD), bf16)
    small = pltpu.VMEM((n, 1, 128), jnp.int32)
    results = pl.pallas_call(
        partial(head_kernel, n, tokens),
        out_shape=[pltpu.VMEM((tokens, width), bf16)] * 4,
        in_specs=[where_it_lies] * 6,
        out_specs=[pl.BlockSpec(memory_space=pltpu.VMEM)] * 4,
        scratch_shapes=[
            *rows,
            pltpu.SMEM((RAND,) + random_blocks.shape[:2], jnp.int32),
            pltpu.VMEM((1, global_positions.shape[0]), jnp.int32),
            whole, folded, folded, small,
            whole, folded, folded, small,
            *([folded] * 8),
            pltpu.VMEM((total, 128), bf16),
            pltpu.VMEM((total, 128), bf16),
            pltpu.VMEM((total, HD), bf16),
            pltpu.VMEM((n, tokens, HD), bf16),
            pltpu.VMEM((n, total, tokens), f32),
            pltpu.VMEM((n, total, tokens), bf16),
            pltpu.VMEM((n, total, tokens), bf16),
            pltpu.SemaphoreType.DMA((6,)),
            pltpu.SemaphoreType.REGULAR,
            pltpu.SemaphoreType.DMA((8, n)),
            pltpu.SemaphoreType.DMA((8, n)),
        ],
        compiler_params=pltpu.CompilerParams(
            collective_id=0, has_side_effects=True, vmem_limit_bytes=LIMIT
        ),
        cost_estimate=pl.CostEstimate(
            flops=14 * total * total * HD, bytes_accessed=16 * tokens * width, transcendentals=total * total
        ),
    )(
        query_rows, key_rows, value_rows, out_grad,
        jnp.transpose(random_blocks, (2, 0, 1)), global_positions.reshape(1, -1),
    )
    return pl.pallas_call(
        write_out,
        out_shape=[jax.ShapeDtypeStruct((tokens, width), bf16)] * 4,
        in_specs=[pl.BlockSpec(memory_space=pltpu.VMEM)] * 4,
        out_specs=[where_it_lies] * 4,
        scratch_shapes=[pltpu.SemaphoreType.DMA((4,))],
    )(*(pltpu.with_memory_space_constraint(r, pltpu.VMEM) for r in results))


def local(query_rows, key_rows, value_rows, out_grad, random_blocks, global_positions):
    n = lax.axis_size("seq")
    tokens = query_rows.shape[0]
    one_head_each = query_rows.shape[1] == n * HD and n > 1
    fits = n == 4 and 8 * n <= 128 - HD and tokens // BLK <= 8 and n * tokens // BLK <= 128
    if one_head_each and fits and tokens % 256 == 0 and n * tokens <= 1024:
        run = local_heads
    else:
        run = local_wide
    return run(query_rows, key_rows, value_rows, out_grad, random_blocks, global_positions)


def solution(mesh):
    placed = (
        P(("groups", "seq"), ("head", "pair")),
        P(("groups", "seq"), ("head", "pair")),
        P(("groups", "seq"), ("head", "pair")),
        P(("groups", "seq"), ("head", "pair")),
        P(("groups", "head", "pair"), "seq", None),
        P("groups"),
    )
    return jax.shard_map(
        local,
        mesh=mesh,
        in_specs=placed,
        out_specs=(
            P(("groups", "seq"), ("head", "pair")),
            P(("groups", "seq"), ("head", "pair")),
            P(("groups", "seq"), ("head", "pair")),
            P(("groups", "seq"), ("head", "pair")),
        ),
        check_vma=False,
    )
```

```python
from functools import partial
import math

import jax
import jax.numpy as jnp
from jax import lax
from jax.experimental import pallas as pl
from jax.experimental.pallas import tpu as pltpu
from jax.sharding import PartitionSpec as P

HD = 64
BLK = 64
RAND = 3


def padded_2(array, sides, width):
    for axis, dim in sides:
        peers, length = (lax.axis_size(axis), array.shape[dim])
        up = [(i, (i + 1) % peers) for i in range(peers - 1)]
        down = [(j, i) for i, j in up]
        last = lax.slice_in_dim(array, length - width, length, axis=dim)
        leading = lax.slice_in_dim(array, 0, width, axis=dim)
        before = lax.ppermute(last, axis, up)
        after = lax.ppermute(leading, axis, down)
        array = jnp.concatenate([before, array, after], axis=dim)
    return array


def from_behind(array, axis, by):
    peers = lax.axis_size(axis)
    pairs = [(i, i + by) for i in range(peers) if 0 <= i + by < peers]
    return lax.ppermute(array, axis, pairs)


def softmax_rows(scores):
    top = jnp.max(scores, axis=-1, keepdims=True)
    raised = jnp.exp(scores - top)
    return raised / jnp.sum(raised, axis=-1, keepdims=True)


def group_probs(query, window, far_rows, global_rows, window_valid, global_keep, scale):
    near = (
        jnp.einsum("bihd,bjhd->bhij", query, window[..., :HD], preferred_element_type=jnp.float32)
        * scale
    )
    far = (
        jnp.einsum("bihd,bjhd->bhij", query, far_rows[..., :HD], preferred_element_type=jnp.float32)
        * scale
    )
    wide = (
        jnp.einsum(
            "bihd,jhd->bhij", query, global_rows[..., :HD], preferred_element_type=jnp.float32
        )
        * scale
    )
    near = jnp.where(window_valid[:, None, None, :], near, -jnp.inf)
    wide = jnp.where(global_keep[:, :, None, :], wide, -jnp.inf)
    return softmax_rows(jnp.concatenate([near, far, wide], axis=-1))


def split_keys(values, window, far_rows):
    span = window.shape[1]
    reach = far_rows.shape[1]
    return (values[..., :span], values[..., span : span + reach], values[..., span + reach :])


def forward_group(items, global_rows, scale):
    query, window, far_rows, window_valid, global_keep = items
    weights = group_probs(
        query, window, far_rows, global_rows, window_valid, global_keep, scale
    ).astype(jnp.bfloat16)
    near, far, wide = split_keys(weights, window, far_rows)
    out = jnp.einsum("bhij,bjhd->bihd", near, window[..., HD:], preferred_element_type=jnp.float32)
    out = out + jnp.einsum(
        "bhij,bjhd->bihd", far, far_rows[..., HD:], preferred_element_type=jnp.float32
    )
    return out + jnp.einsum(
        "bhij,jhd->bihd", wide, global_rows[..., HD:], preferred_element_type=jnp.float32
    )


def backward_group(items, global_rows, scale):
    query, window, far_rows, window_valid, global_keep, grad_out, delta = items
    probs = group_probs(query, window, far_rows, global_rows, window_valid, global_keep, scale)
    weights = probs.astype(jnp.bfloat16)
    value_dot = jnp.concatenate(
        [
            jnp.einsum(
                "bihd,bjhd->bhij", grad_out, window[..., HD:], preferred_element_type=jnp.float32
            ),
            jnp.einsum(
                "bihd,bjhd->bhij", grad_out, far_rows[..., HD:], preferred_element_type=jnp.float32
            ),
            jnp.einsum(
                "bihd,jhd->bhij",
                grad_out,
                global_rows[..., HD:],
                preferred_element_type=jnp.float32,
            ),
        ],
        axis=-1,
    )
    dscore = (probs * (value_dot - jnp.transpose(delta, (0, 2, 1))[..., None])).astype(jnp.bfloat16)
    dnear, dfar, dwide = split_keys(dscore, window, far_rows)
    near, far, wide = split_keys(weights, window, far_rows)
    grad_query = jnp.einsum(
        "bhij,bjhd->bihd", dnear, window[..., :HD], preferred_element_type=jnp.float32
    )
    grad_query = grad_query + jnp.einsum(
        "bhij,bjhd->bihd", dfar, far_rows[..., :HD], preferred_element_type=jnp.float32
    )
    grad_query = scale * (
        grad_query
        + jnp.einsum(
            "bhij,jhd->bihd", dwide, global_rows[..., :HD], preferred_element_type=jnp.float32
        )
    )
    grad_window = jnp.concatenate(
        [
            scale * jnp.einsum("bhij,bihd->bjhd", dnear, query, preferred_element_type=jnp.float32),
            jnp.einsum("bhij,bihd->bjhd", near, grad_out, preferred_element_type=jnp.float32),
        ],
        axis=-1,
    )
    grad_far = jnp.concatenate(
        [
            scale * jnp.einsum("bhij,bihd->bjhd", dfar, query, preferred_element_type=jnp.float32),
            jnp.einsum("bhij,bihd->bjhd", far, grad_out, preferred_element_type=jnp.float32),
        ],
        axis=-1,
    ).astype(jnp.bfloat16)
    grad_wide = jnp.concatenate(
        [
            scale * jnp.einsum("bhij,bihd->jhd", dwide, query, preferred_element_type=jnp.float32),
            jnp.einsum("bhij,bihd->jhd", wide, grad_out, preferred_element_type=jnp.float32),
        ],
        axis=-1,
    )
    return (grad_query, grad_window, grad_far, grad_wide)


def local_wide(query_rows, key_rows, value_rows, out_grad, random_blocks, global_positions):
    tokens = query_rows.shape[0]
    heads = query_rows.shape[1] // HD
    blocks = tokens // BLK
    devices = lax.axis_size("seq")
    place = lax.axis_index("seq")
    scale = 1.0 / math.sqrt(HD)
    capacity = RAND * (blocks // (devices - 1)) + min(RAND, blocks % (devices - 1))
    group = math.gcd(blocks, max(1, 512 // BLK))
    count = blocks // group
    local_index = global_positions - place * tokens
    owned = (local_index >= 0) & (local_index < tokens)
    target = jnp.where(owned, local_index, tokens)
    safe_index = jnp.where(owned, local_index, 0)

    def pick(rows):
        return jnp.where(owned[:, None], rows[safe_index].astype(jnp.float32), 0.0)

    glob_sum = (
        lax.psum(pick(query_rows).astype(jnp.bfloat16), "seq").astype(jnp.float32),
        lax.psum(pick(key_rows).astype(jnp.bfloat16), "seq").astype(jnp.float32),
        lax.psum(pick(value_rows).astype(jnp.bfloat16), "seq").astype(jnp.float32),
        lax.psum(pick(out_grad).astype(jnp.bfloat16), "seq").astype(jnp.float32),
    )
    glob_query = glob_sum[0].astype(jnp.bfloat16).reshape(-1, heads, HD)
    glob_key = glob_sum[1].astype(jnp.bfloat16).reshape(-1, heads, HD)
    glob_value = glob_sum[2].astype(jnp.bfloat16).reshape(-1, heads, HD)
    glob_grad = glob_sum[3].astype(jnp.bfloat16).reshape(-1, heads, HD)
    global_rows = jnp.concatenate([glob_key, glob_value], axis=-1)
    query3 = query_rows.reshape(tokens, heads, HD)
    key3 = key_rows.reshape(tokens, heads, HD)
    value3 = value_rows.reshape(tokens, heads, HD)
    pair_rows = jnp.concatenate([key3, value3], axis=-1)
    padded = padded_2(pair_rows, (("seq", 0),), BLK)
    framed = padded.reshape(blocks + 2, BLK, heads, 2 * HD)
    window = jnp.concatenate([framed[:-2], framed[1:-1], framed[2:]], axis=1)
    block_ids = place * blocks + jnp.arange(blocks)
    neighbour = block_ids[:, None] + (jnp.repeat(jnp.arange(3), BLK) - 1)[None, :]
    window_valid = (neighbour >= 0) & (neighbour < devices * blocks)
    global_block = global_positions // BLK
    near_glob = jnp.abs(global_block[None, :] - block_ids[:, None]) <= 1
    in_random = jnp.any(random_blocks[:, :, :, None] == global_block[None, None, None, :], axis=2)
    global_keep = jnp.logical_not(near_glob[:, None, :] | jnp.transpose(in_random, (1, 0, 2)))
    owner = random_blocks // blocks
    local_block = random_blocks % blocks
    flat_owner = owner.reshape(heads, blocks * RAND)
    hits = (flat_owner[:, :, None] == jnp.arange(devices)[None, None, :]).astype(jnp.int32)
    before = jnp.cumsum(hits, axis=1) - hits
    flat_slot = jnp.sum(before * hits, axis=2)
    placed = (flat_slot[:, :, None] == jnp.arange(capacity)[None, None, :]).astype(jnp.int32)
    marks = (local_block.reshape(heads, blocks * RAND) + 1)[:, :, None, None]
    table = jnp.sum(hits[:, :, :, None] * placed[:, :, None, :] * marks, axis=1) - 1
    asked = lax.all_to_all(
        jnp.transpose(table, (1, 0, 2)), "seq", split_axis=0, concat_axis=0, tiled=True
    )
    own_blocks = pair_rows.reshape(blocks, BLK, heads, 2 * HD)
    wanted = (jnp.maximum(asked, 0)[..., None] == jnp.arange(blocks)).astype(jnp.bfloat16)
    served = jnp.einsum(
        "zhcb,bthf->zhctf", wanted, own_blocks, preferred_element_type=jnp.float32
    ).astype(jnp.bfloat16)
    owner_order = jnp.transpose(owner, (1, 2, 0))
    slot_order = jnp.transpose(flat_slot.reshape(heads, blocks, RAND), (1, 2, 0))
    head_order = jnp.arange(heads)[None, None, :]
    arrived = lax.all_to_all(served, "seq", split_axis=0, concat_axis=0, tiled=True)
    arrived = jnp.transpose(arrived, (0, 2, 1, 3, 4)).reshape(
        devices * capacity, heads, BLK, 2 * HD
    )
    source = owner_order * capacity + slot_order
    chosen = (source[..., None] == jnp.arange(devices * capacity)).astype(jnp.bfloat16)
    picked = jnp.einsum(
        "brhz,zhtf->brhtf", chosen, arrived, preferred_element_type=jnp.float32
    ).astype(jnp.bfloat16)
    far_rows = jnp.transpose(picked, (0, 1, 3, 2, 4)).reshape(blocks, RAND * BLK, heads, 2 * HD)

    def grouped(array):
        return array.reshape((count, group) + array.shape[1:])

    query_blocks = query3.reshape(blocks, BLK, heads, HD)
    sparse_out = lax.map(
        partial(forward_group, global_rows=global_rows, scale=scale),
        (
            grouped(query_blocks),
            grouped(window),
            grouped(far_rows),
            grouped(window_valid),
            grouped(global_keep),
        ),
    )
    sparse_out = sparse_out.reshape(tokens, heads, HD)
    wide = jnp.einsum("ghd,thd->hgt", glob_query, key3, preferred_element_type=jnp.float32) * scale
    local_top = jnp.max(wide, axis=-1)
    top = lax.pmax(local_top, "seq")
    total = lax.psum(jnp.sum(jnp.exp(wide - top[..., None]), axis=-1), "seq")
    glob_probs = jnp.exp(wide - top[..., None]) / total[..., None]
    glob_weights = glob_probs.astype(jnp.bfloat16)
    glob_part = jnp.einsum("hgt,thd->ghd", glob_weights, value3, preferred_element_type=jnp.float32)
    glob_out = lax.psum(glob_part, "seq").astype(jnp.bfloat16)
    attended = sparse_out.astype(jnp.bfloat16).at[target].set(glob_out, mode="drop")
    glob_mask = jnp.zeros((tokens,), jnp.bool_).at[target].set(True, mode="drop")
    sparse_grad = jnp.where(
        glob_mask[:, None, None],
        jnp.zeros_like(out_grad.reshape(tokens, heads, HD)),
        out_grad.reshape(tokens, heads, HD),
    )
    delta = jnp.sum(sparse_grad.astype(jnp.float32) * attended.astype(jnp.float32), axis=-1)
    grad_query, grad_window, grad_far, grad_wide = lax.map(
        partial(backward_group, global_rows=global_rows, scale=scale),
        (
            grouped(query_blocks),
            grouped(window),
            grouped(far_rows),
            grouped(window_valid),
            grouped(global_keep),
            grouped(sparse_grad.reshape(blocks, BLK, heads, HD)),
            grouped(delta.reshape(blocks, BLK, heads)),
        ),
    )
    grad_query = grad_query.reshape(tokens, heads, HD)
    grad_window = grad_window.reshape(blocks, 3, BLK, heads, 2 * HD)
    grad_wide = jnp.sum(grad_wide, axis=0)
    folded = jnp.zeros((blocks + 2, BLK, heads, 2 * HD), jnp.float32)
    folded = (
        folded.at[0:blocks]
        .add(grad_window[:, 0])
        .at[1 : blocks + 1]
        .add(grad_window[:, 1])
        .at[2 : blocks + 2]
        .add(grad_window[:, 2])
    )
    from_right = from_behind(folded[0], "seq", -1)
    from_left = from_behind(folded[blocks + 1], "seq", 1)
    local_pair = folded[1 : blocks + 1]
    local_pair = local_pair.at[blocks - 1].add(from_right).at[0].add(from_left)
    far_terms = jnp.transpose(grad_far.reshape(blocks, RAND, BLK, heads, 2 * HD), (0, 1, 3, 2, 4))
    outgoing = (
        jnp.zeros((devices, heads, capacity, BLK, 2 * HD), jnp.bfloat16)
        .at[owner_order, head_order, slot_order]
        .set(far_terms)
    )
    returned = lax.all_to_all(outgoing, "seq", split_axis=0, concat_axis=0, tiled=True)
    landing = jnp.where(asked >= 0, asked, blocks)
    gathered = (
        jnp.zeros((blocks, heads, BLK, 2 * HD), jnp.float32)
        .at[landing, jnp.arange(heads)[None, :, None]]
        .add(returned.astype(jnp.float32), mode="drop")
    )
    pair_grad = local_pair.reshape(tokens, heads, 2 * HD) + jnp.transpose(
        gathered, (0, 2, 1, 3)
    ).reshape(tokens, heads, 2 * HD)
    glob_attended = glob_out.astype(jnp.float32)
    glob_delta = jnp.sum(glob_grad.astype(jnp.float32) * glob_attended, axis=-1)
    glob_dot = jnp.einsum("ghd,thd->hgt", glob_grad, value3, preferred_element_type=jnp.float32)
    glob_dscore = (glob_probs * (glob_dot - jnp.transpose(glob_delta)[..., None])).astype(
        jnp.bfloat16
    )
    query_part = scale * jnp.einsum(
        "hgt,thd->ghd", glob_dscore, key3, preferred_element_type=jnp.float32
    )
    key_from_glob = scale * jnp.einsum(
        "hgt,ghd->thd", glob_dscore, glob_query, preferred_element_type=jnp.float32
    )
    value_from_glob = jnp.einsum(
        "hgt,ghd->thd", glob_weights, glob_grad, preferred_element_type=jnp.float32
    )
    summed = lax.psum((query_part, grad_wide), "seq")
    grad_query = grad_query.at[target].add(summed[0], mode="drop")
    pair_grad = pair_grad.at[target].add(summed[1], mode="drop")
    grad_key = pair_grad[..., :HD] + key_from_glob
    grad_value = pair_grad[..., HD:] + value_from_glob
    return (
        attended.reshape(tokens, heads * HD),
        grad_query.reshape(tokens, heads * HD).astype(jnp.bfloat16),
        grad_key.reshape(tokens, heads * HD).astype(jnp.bfloat16),
        grad_value.reshape(tokens, heads * HD).astype(jnp.bfloat16),
    )


BIG = 1e30
LIMIT = 63 * 1024 * 1024
NT = (((1,), (1,)), ((), ()))
TN = (((0,), (0,)), ((), ()))
NN = (((1,), (0,)), ((), ()))


def mm(left, right, dims):
    return lax.dot_general(left, right, dims, preferred_element_type=jnp.float32)


def head_kernel(
    n, tokens, q_hbm, k_hbm, v_hbm, g_hbm, rb_hbm, gp_hbm, att_ref, dq_ref, dk_ref, dv_ref,
    q_ref, k_ref, v_ref, g_ref, rb_ref, gp_ref, kq_send, v_send, g_send, tab_send, kq, vp, gp, tab,
    att_send, dv_send, dq_send, dk_send, att, dv, dq, dk,
    ka, qa, va, ga, probs, weights, dscore, load_sem, turn, send_sem, recv_sem,
):
    me = lax.axis_index("seq")
    total = n * tokens
    part = tokens // 2
    qb = tokens // BLK
    scale = 1.0 / math.sqrt(HD)
    half = me // 2
    inner = (me % 3 + 1) // 2
    near, far, mate = 2 - 2 * half, 3 - 2 * half, 1 - me + 4 * half
    others = [
        inner * mate + (1 - inner) * near,
        inner * near + (1 - inner) * far,
        inner * far + (1 - inner) * mate,
    ]

    barrier = pltpu.get_barrier_semaphore()
    for peer in others:
        pl.semaphore_signal(
            barrier, inc=1, device_id={"seq": peer}, device_id_type=pl.DeviceIdType.MESH
        )
    loads = [
        pltpu.make_async_copy(hbm, vmem, load_sem.at[i])
        for i, (hbm, vmem) in enumerate(
            ((k_hbm, k_ref), (q_hbm, q_ref), (v_hbm, v_ref), (g_hbm, g_ref), (rb_hbm, rb_ref), (gp_hbm, gp_ref))
        )
    ]
    for i in (4, 0, 1, 2, 3, 5):
        loads[i].start()

    stages = (
        (tab_send, tab), (kq_send, kq), (v_send, vp), (g_send, gp),
        (att_send, att), (dv_send, dv), (dq_send, dq), (dk_send, dk),
    )

    def copy(stage, peer, slot):
        send, recv = stages[stage]
        return pltpu.make_async_remote_copy(
            src_ref=send.at[peer],
            dst_ref=recv.at[slot],
            send_sem=send_sem.at[stage, peer],
            recv_sem=recv_sem.at[stage, slot],
            device_id={"seq": peer},
            device_id_type=pl.DeviceIdType.MESH,
        )

    def start(stage, peer):
        copy(stage, peer, me).start()

    def arrive(stage):
        for peer in others:
            copy(stage, peer, peer).wait_recv()

    def keep(stage):
        send, recv = stages[stage]
        recv[me] = send[me]

    def fold(ref, slot, rows):
        ref[slot, :, 0:HD] = rows[0:part]
        ref[slot, :, HD : 2 * HD] = rows[part:tokens]

    def fold_t(ref, slot, columns):
        stacked = jnp.concatenate([columns[:, 0:part], columns[:, part:tokens]], axis=0)
        ref[slot] = stacked.T.astype(jnp.bfloat16)

    lane = lax.broadcasted_iota(jnp.int32, (1, 128), 1)
    loads[4].wait()
    for h in range(n):
        mark = jnp.zeros((1, 128), jnp.int32)
        for r in range(RAND):
            for b in range(qb):
                at = lax.rem(HD + r * 8 * n + 8 * me + b, 128)
                mark = jnp.where(lane == at, rb_ref[r, h, b], mark)
        tab_send[h] = mark
    loads[0].wait()
    loads[1].wait()
    for h in range(n):
        cols = slice(h * HD, (h + 1) * HD)
        kq_send[h, :, 0:HD] = k_ref[:, cols]
        kq_send[h, :, HD : 2 * HD] = q_ref[:, cols] * jnp.bfloat16(scale)
    pl.semaphore_wait(barrier, n - 1)
    @pl.when(inner == 1)
    def _():
        for peer in others:
            start(0, peer)
            start(1, peer)

    loads[2].wait()
    for h in range(n):
        fold(v_send, h, v_ref[:, h * HD : (h + 1) * HD])
    loads[3].wait()
    for h in range(n):
        fold(g_send, h, g_ref[:, h * HD : (h + 1) * HD])

    @pl.when(inner == 1)
    def _():
        for stage in (2, 3):
            for peer in others:
                start(stage, peer)
        copy(1, mate, me).wait_send()
        pl.semaphore_signal(turn, inc=1, device_id={"seq": mate}, device_id_type=pl.DeviceIdType.MESH)

    pos = lax.broadcasted_iota(jnp.int32, (total, 128), 0)
    col = lax.broadcasted_iota(jnp.int32, (total, 128), 1)
    loads[5].wait()
    globals_here = gp_ref.shape[1]
    spots = lax.broadcasted_iota(jnp.int32, (total, globals_here), 0) == gp_ref[...]
    spread = mm(
        jnp.where(spots, 1.0, 0.0).astype(jnp.bfloat16),
        jnp.ones((globals_here, 128), jnp.bfloat16),
        NN,
    )
    is_global = spread > 0.5
    slot = col - HD
    block = (slot // 8) * qb + slot % 8
    mine = (slot >= 0) & (slot < 8 * n) & (slot % 8 < qb)
    key_block = pos // BLK
    window = mine & (block - key_block <= 1) & (key_block - block <= 1)
    open_key = window | is_global
    hot = jnp.where(mine & (block == key_block) & jnp.logical_not(is_global), 1.0, 0.0)

    @pl.when(inner == 0)
    def _():
        pl.semaphore_wait(turn, 1)
        for stage in (0, 1, 2):
            for peer in others:
                start(stage, peer)

    for stage in range(4):
        keep(stage)

    @pl.when(inner == 0)
    def _():
        copy(2, far, me).wait_send()
        for peer in others:
            start(3, peer)

    arrive(0)
    picks = tab[0]
    for c in range(1, n):
        picks = picks + tab[c]
    for r in range(RAND):
        shifted = picks if r == 0 else pltpu.roll(picks, 128 - r * 8 * n, 1)
        open_key = open_key | (mine & (key_block == shifted))
    bias = jnp.where(open_key, 0.0, -BIG).astype(jnp.bfloat16)
    arrive(1)
    pair = kq[...].reshape(total, 128)
    ka[...] = bias
    ka[:, 0:HD] = pair[:, 0:HD]
    qa[...] = hot.astype(jnp.bfloat16)
    qa[:, 0:HD] = pair[:, HD : 2 * HD]

    keys = ka[...]
    for a in range(n):
        score = mm(keys, qa[a * tokens : (a + 1) * tokens, :], NT)
        top = jnp.max(score, axis=0, keepdims=True)
        raised = jnp.exp(score - top)
        prob = raised * (1.0 / jnp.sum(raised, axis=0, keepdims=True))
        probs[a] = prob
        weights[a] = prob.astype(jnp.bfloat16)
    keys_t = keys[:, 0:HD].T

    order = others + [me]
    arrive(2)
    for c in range(n):
        va[c * tokens : c * tokens + part, :] = vp[c, :, 0:HD]
        va[c * tokens + part : (c + 1) * tokens, :] = vp[c, :, HD : 2 * HD]
    values = va[...]
    values_t = values.T
    outs = []
    for a in order:
        out = mm(values_t, weights[a], NN)
        fold_t(att_send, a, out)
        if a is not me and a is not others[2]:
            start(4, a)
        outs.append(out.astype(jnp.bfloat16).astype(jnp.float32))

    arrive(3)
    for c in range(n):
        ga[c, 0:part, :] = gp[c, :, 0:HD]
        ga[c, part:tokens, :] = gp[c, :, HD : 2 * HD]

    def value_grad(a):
        rows = pl.ds(pl.multiple_of(a * tokens, tokens), tokens)
        grad = jnp.zeros((tokens, HD), jnp.float32)
        for c in range(n):
            grad = grad + mm(weights[c, rows, :], ga[c], NN)
        fold(dv_send, a, grad.astype(jnp.bfloat16))

    def score_grad(a, out):
        grad = ga[a]
        delta = jnp.sum(grad.astype(jnp.float32).T * out, axis=0, keepdims=True)
        dprob = mm(values, grad, NT)
        dscore[a] = (probs[a] * (dprob - delta)).astype(jnp.bfloat16)

    def query_grad(a):
        fold_t(dq_send, a, mm(keys_t, dscore[a], NN) * scale)

    def key_grad(a):
        rows = pl.ds(pl.multiple_of(a * tokens, tokens), tokens)
        grad = jnp.zeros((tokens, HD), jnp.float32)
        for c in range(n):
            grad = grad + mm(dscore[c, rows, :], qa[c * tokens : (c + 1) * tokens, 0:HD], NN)
        fold(dk_send, a, grad.astype(jnp.bfloat16))

    value_grad(order[0])
    start(5, order[0])
    value_grad(order[1])
    start(5, order[1])
    score_grad(order[0], outs[0])
    query_grad(order[0])
    start(6, order[0])
    score_grad(order[1], outs[1])
    score_grad(order[2], outs[2])
    score_grad(order[3], outs[3])
    key_grad(order[0])
    start(7, order[0])
    query_grad(order[1])
    start(6, order[1])
    key_grad(order[1])
    start(7, order[1])
    start(4, order[2])
    value_grad(order[2])
    start(5, order[2])
    query_grad(order[2])
    start(6, order[2])
    key_grad(order[2])
    start(7, order[2])
    value_grad(order[3])
    query_grad(order[3])
    key_grad(order[3])
    for stage in range(4, 8):
        keep(stage)

    for stage, ref in ((4, att_ref), (5, dv_ref), (6, dq_ref), (7, dk_ref)):
        arrive(stage)
        recv = stages[stage][1]
        for h in range(n):
            cols = slice(h * HD, (h + 1) * HD)
            ref[0:part, cols] = recv[h, :, 0:HD]
            ref[part:tokens, cols] = recv[h, :, HD : 2 * HD]
    @pl.when(inner == 1)
    def _():
        copy(2, far, me).wait_send()

    @pl.when(inner == 0)
    def _():
        copy(1, mate, me).wait_send()

    for stage in range(len(stages)):
        for peer in (near, far) if stage == 1 else (mate, near) if stage == 2 else others:
            copy(stage, peer, me).wait_send()


def write_out(*refs):
    count = len(refs) // 2
    sources, targets, sem = refs[:count], refs[count : 2 * count], refs[-1]
    stores = [pltpu.make_async_copy(sources[i], targets[i], sem.at[i]) for i in range(count)]
    for store in stores:
        store.start()
    for store in stores:
        store.wait()


def local_heads(query_rows, key_rows, value_rows, out_grad, random_blocks, global_positions):
    tokens, width = query_rows.shape
    n = lax.axis_size("seq")
    total = n * tokens
    bf16, f32 = jnp.bfloat16, jnp.float32
    where_it_lies = pl.BlockSpec(memory_space=pltpu.HBM)
    rows = [pltpu.VMEM((tokens, width), bf16)] * 4
    whole = pltpu.VMEM((n, tokens, 2 * HD), bf16)
    folded = pltpu.VMEM((n, tokens // 2, 2 * HD), bf16)
    small = pltpu.VMEM((n, 1, 128), jnp.int32)
    results = pl.pallas_call(
        partial(head_kernel, n, tokens),
        out_shape=[pltpu.VMEM((tokens, width), bf16)] * 4,
        in_specs=[where_it_lies] * 6,
        out_specs=[pl.BlockSpec(memory_space=pltpu.VMEM)] * 4,
        scratch_shapes=[
            *rows,
            pltpu.SMEM((RAND,) + random_blocks.shape[:2], jnp.int32),
            pltpu.VMEM((1, global_positions.shape[0]), jnp.int32),
            whole, folded, folded, small,
            whole, folded, folded, small,
            *([folded] * 8),
            pltpu.VMEM((total, 128), bf16),
            pltpu.VMEM((total, 128), bf16),
            pltpu.VMEM((total, HD), bf16),
            pltpu.VMEM((n, tokens, HD), bf16),
            pltpu.VMEM((n, total, tokens), f32),
            pltpu.VMEM((n, total, tokens), bf16),
            pltpu.VMEM((n, total, tokens), bf16),
            pltpu.SemaphoreType.DMA((6,)),
            pltpu.SemaphoreType.REGULAR,
            pltpu.SemaphoreType.DMA((8, n)),
            pltpu.SemaphoreType.DMA((8, n)),
        ],
        compiler_params=pltpu.CompilerParams(
            collective_id=0, has_side_effects=True, vmem_limit_bytes=LIMIT
        ),
        cost_estimate=pl.CostEstimate(
            flops=14 * total * total * HD, bytes_accessed=16 * tokens * width, transcendentals=total * total
        ),
    )(
        query_rows, key_rows, value_rows, out_grad,
        jnp.transpose(random_blocks, (2, 0, 1)), global_positions.reshape(1, -1),
    )
    return pl.pallas_call(
        write_out,
        out_shape=[jax.ShapeDtypeStruct((tokens, width), bf16)] * 4,
        in_specs=[pl.BlockSpec(memory_space=pltpu.VMEM)] * 4,
        out_specs=[where_it_lies] * 4,
        scratch_shapes=[pltpu.SemaphoreType.DMA((4,))],
    )(*(pltpu.with_memory_space_constraint(r, pltpu.VMEM) for r in results))


def local(query_rows, key_rows, value_rows, out_grad, random_blocks, global_positions):
    n = lax.axis_size("seq")
    tokens = query_rows.shape[0]
    one_head_each = query_rows.shape[1] == n * HD and n > 1
    fits = n == 4 and 8 * n <= 128 - HD and tokens // BLK <= 8 and n * tokens // BLK <= 128
    if one_head_each and fits and tokens % 256 == 0 and n * tokens <= 1024:
        run = local_heads
    else:
        run = local_wide
    return run(query_rows, key_rows, value_rows, out_grad, random_blocks, global_positions)


def solution(mesh):
    placed = (
        P(("groups", "seq"), ("head", "pair")),
        P(("groups", "seq"), ("head", "pair")),
        P(("groups", "seq"), ("head", "pair")),
        P(("groups", "seq"), ("head", "pair")),
        P(("groups", "head", "pair"), "seq", None),
        P("groups"),
    )
    return jax.shard_map(
        local,
        mesh=mesh,
        in_specs=placed,
        out_specs=(
            P(("groups", "seq"), ("head", "pair")),
            P(("groups", "seq"), ("head", "pair")),
            P(("groups", "seq"), ("head", "pair")),
            P(("groups", "seq"), ("head", "pair")),
        ),
        check_vma=False,
    )
```

```python
from functools import partial
import math

import jax
import jax.numpy as jnp
from jax import lax
from jax.experimental import pallas as pl
from jax.experimental.pallas import tpu as pltpu
from jax.sharding import PartitionSpec as P

HD = 64
BLK = 64
RAND = 3


def padded_2(array, sides, width):
    for axis, dim in sides:
        peers, length = (lax.axis_size(axis), array.shape[dim])
        up = [(i, (i + 1) % peers) for i in range(peers - 1)]
        down = [(j, i) for i, j in up]
        last = lax.slice_in_dim(array, length - width, length, axis=dim)
        leading = lax.slice_in_dim(array, 0, width, axis=dim)
        before = lax.ppermute(last, axis, up)
        after = lax.ppermute(leading, axis, down)
        array = jnp.concatenate([before, array, after], axis=dim)
    return array


def from_behind(array, axis, by):
    peers = lax.axis_size(axis)
    pairs = [(i, i + by) for i in range(peers) if 0 <= i + by < peers]
    return lax.ppermute(array, axis, pairs)


def softmax_rows(scores):
    top = jnp.max(scores, axis=-1, keepdims=True)
    raised = jnp.exp(scores - top)
    return raised / jnp.sum(raised, axis=-1, keepdims=True)


def group_probs(query, window, far_rows, global_rows, window_valid, global_keep, scale):
    near = (
        jnp.einsum("bihd,bjhd->bhij", query, window[..., :HD], preferred_element_type=jnp.float32)
        * scale
    )
    far = (
        jnp.einsum("bihd,bjhd->bhij", query, far_rows[..., :HD], preferred_element_type=jnp.float32)
        * scale
    )
    wide = (
        jnp.einsum(
            "bihd,jhd->bhij", query, global_rows[..., :HD], preferred_element_type=jnp.float32
        )
        * scale
    )
    near = jnp.where(window_valid[:, None, None, :], near, -jnp.inf)
    wide = jnp.where(global_keep[:, :, None, :], wide, -jnp.inf)
    return softmax_rows(jnp.concatenate([near, far, wide], axis=-1))


def split_keys(values, window, far_rows):
    span = window.shape[1]
    reach = far_rows.shape[1]
    return (values[..., :span], values[..., span : span + reach], values[..., span + reach :])


def forward_group(items, global_rows, scale):
    query, window, far_rows, window_valid, global_keep = items
    weights = group_probs(
        query, window, far_rows, global_rows, window_valid, global_keep, scale
    ).astype(jnp.bfloat16)
    near, far, wide = split_keys(weights, window, far_rows)
    out = jnp.einsum("bhij,bjhd->bihd", near, window[..., HD:], preferred_element_type=jnp.float32)
    out = out + jnp.einsum(
        "bhij,bjhd->bihd", far, far_rows[..., HD:], preferred_element_type=jnp.float32
    )
    return out + jnp.einsum(
        "bhij,jhd->bihd", wide, global_rows[..., HD:], preferred_element_type=jnp.float32
    )


def backward_group(items, global_rows, scale):
    query, window, far_rows, window_valid, global_keep, grad_out, delta = items
    probs = group_probs(query, window, far_rows, global_rows, window_valid, global_keep, scale)
    weights = probs.astype(jnp.bfloat16)
    value_dot = jnp.concatenate(
        [
            jnp.einsum(
                "bihd,bjhd->bhij", grad_out, window[..., HD:], preferred_element_type=jnp.float32
            ),
            jnp.einsum(
                "bihd,bjhd->bhij", grad_out, far_rows[..., HD:], preferred_element_type=jnp.float32
            ),
            jnp.einsum(
                "bihd,jhd->bhij",
                grad_out,
                global_rows[..., HD:],
                preferred_element_type=jnp.float32,
            ),
        ],
        axis=-1,
    )
    dscore = (probs * (value_dot - jnp.transpose(delta, (0, 2, 1))[..., None])).astype(jnp.bfloat16)
    dnear, dfar, dwide = split_keys(dscore, window, far_rows)
    near, far, wide = split_keys(weights, window, far_rows)
    grad_query = jnp.einsum(
        "bhij,bjhd->bihd", dnear, window[..., :HD], preferred_element_type=jnp.float32
    )
    grad_query = grad_query + jnp.einsum(
        "bhij,bjhd->bihd", dfar, far_rows[..., :HD], preferred_element_type=jnp.float32
    )
    grad_query = scale * (
        grad_query
        + jnp.einsum(
            "bhij,jhd->bihd", dwide, global_rows[..., :HD], preferred_element_type=jnp.float32
        )
    )
    grad_window = jnp.concatenate(
        [
            scale * jnp.einsum("bhij,bihd->bjhd", dnear, query, preferred_element_type=jnp.float32),
            jnp.einsum("bhij,bihd->bjhd", near, grad_out, preferred_element_type=jnp.float32),
        ],
        axis=-1,
    )
    grad_far = jnp.concatenate(
        [
            scale * jnp.einsum("bhij,bihd->bjhd", dfar, query, preferred_element_type=jnp.float32),
            jnp.einsum("bhij,bihd->bjhd", far, grad_out, preferred_element_type=jnp.float32),
        ],
        axis=-1,
    ).astype(jnp.bfloat16)
    grad_wide = jnp.concatenate(
        [
            scale * jnp.einsum("bhij,bihd->jhd", dwide, query, preferred_element_type=jnp.float32),
            jnp.einsum("bhij,bihd->jhd", wide, grad_out, preferred_element_type=jnp.float32),
        ],
        axis=-1,
    )
    return (grad_query, grad_window, grad_far, grad_wide)


def local_wide(query_rows, key_rows, value_rows, out_grad, random_blocks, global_positions):
    tokens = query_rows.shape[0]
    heads = query_rows.shape[1] // HD
    blocks = tokens // BLK
    devices = lax.axis_size("seq")
    place = lax.axis_index("seq")
    scale = 1.0 / math.sqrt(HD)
    capacity = RAND * (blocks // (devices - 1)) + min(RAND, blocks % (devices - 1))
    group = math.gcd(blocks, max(1, 512 // BLK))
    count = blocks // group
    local_index = global_positions - place * tokens
    owned = (local_index >= 0) & (local_index < tokens)
    target = jnp.where(owned, local_index, tokens)
    safe_index = jnp.where(owned, local_index, 0)

    def pick(rows):
        return jnp.where(owned[:, None], rows[safe_index].astype(jnp.float32), 0.0)

    glob_sum = (
        lax.psum(pick(query_rows).astype(jnp.bfloat16), "seq").astype(jnp.float32),
        lax.psum(pick(key_rows).astype(jnp.bfloat16), "seq").astype(jnp.float32),
        lax.psum(pick(value_rows).astype(jnp.bfloat16), "seq").astype(jnp.float32),
        lax.psum(pick(out_grad).astype(jnp.bfloat16), "seq").astype(jnp.float32),
    )
    glob_query = glob_sum[0].astype(jnp.bfloat16).reshape(-1, heads, HD)
    glob_key = glob_sum[1].astype(jnp.bfloat16).reshape(-1, heads, HD)
    glob_value = glob_sum[2].astype(jnp.bfloat16).reshape(-1, heads, HD)
    glob_grad = glob_sum[3].astype(jnp.bfloat16).reshape(-1, heads, HD)
    global_rows = jnp.concatenate([glob_key, glob_value], axis=-1)
    query3 = query_rows.reshape(tokens, heads, HD)
    key3 = key_rows.reshape(tokens, heads, HD)
    value3 = value_rows.reshape(tokens, heads, HD)
    pair_rows = jnp.concatenate([key3, value3], axis=-1)
    padded = padded_2(pair_rows, (("seq", 0),), BLK)
    framed = padded.reshape(blocks + 2, BLK, heads, 2 * HD)
    window = jnp.concatenate([framed[:-2], framed[1:-1], framed[2:]], axis=1)
    block_ids = place * blocks + jnp.arange(blocks)
    neighbour = block_ids[:, None] + (jnp.repeat(jnp.arange(3), BLK) - 1)[None, :]
    window_valid = (neighbour >= 0) & (neighbour < devices * blocks)
    global_block = global_positions // BLK
    near_glob = jnp.abs(global_block[None, :] - block_ids[:, None]) <= 1
    in_random = jnp.any(random_blocks[:, :, :, None] == global_block[None, None, None, :], axis=2)
    global_keep = jnp.logical_not(near_glob[:, None, :] | jnp.transpose(in_random, (1, 0, 2)))
    owner = random_blocks // blocks
    local_block = random_blocks % blocks
    flat_owner = owner.reshape(heads, blocks * RAND)
    hits = (flat_owner[:, :, None] == jnp.arange(devices)[None, None, :]).astype(jnp.int32)
    before = jnp.cumsum(hits, axis=1) - hits
    flat_slot = jnp.sum(before * hits, axis=2)
    placed = (flat_slot[:, :, None] == jnp.arange(capacity)[None, None, :]).astype(jnp.int32)
    marks = (local_block.reshape(heads, blocks * RAND) + 1)[:, :, None, None]
    table = jnp.sum(hits[:, :, :, None] * placed[:, :, None, :] * marks, axis=1) - 1
    asked = lax.all_to_all(
        jnp.transpose(table, (1, 0, 2)), "seq", split_axis=0, concat_axis=0, tiled=True
    )
    own_blocks = pair_rows.reshape(blocks, BLK, heads, 2 * HD)
    wanted = (jnp.maximum(asked, 0)[..., None] == jnp.arange(blocks)).astype(jnp.bfloat16)
    served = jnp.einsum(
        "zhcb,bthf->zhctf", wanted, own_blocks, preferred_element_type=jnp.float32
    ).astype(jnp.bfloat16)
    owner_order = jnp.transpose(owner, (1, 2, 0))
    slot_order = jnp.transpose(flat_slot.reshape(heads, blocks, RAND), (1, 2, 0))
    head_order = jnp.arange(heads)[None, None, :]
    arrived = lax.all_to_all(served, "seq", split_axis=0, concat_axis=0, tiled=True)
    arrived = jnp.transpose(arrived, (0, 2, 1, 3, 4)).reshape(
        devices * capacity, heads, BLK, 2 * HD
    )
    source = owner_order * capacity + slot_order
    chosen = (source[..., None] == jnp.arange(devices * capacity)).astype(jnp.bfloat16)
    picked = jnp.einsum(
        "brhz,zhtf->brhtf", chosen, arrived, preferred_element_type=jnp.float32
    ).astype(jnp.bfloat16)
    far_rows = jnp.transpose(picked, (0, 1, 3, 2, 4)).reshape(blocks, RAND * BLK, heads, 2 * HD)

    def grouped(array):
        return array.reshape((count, group) + array.shape[1:])

    query_blocks = query3.reshape(blocks, BLK, heads, HD)
    sparse_out = lax.map(
        partial(forward_group, global_rows=global_rows, scale=scale),
        (
            grouped(query_blocks),
            grouped(window),
            grouped(far_rows),
            grouped(window_valid),
            grouped(global_keep),
        ),
    )
    sparse_out = sparse_out.reshape(tokens, heads, HD)
    wide = jnp.einsum("ghd,thd->hgt", glob_query, key3, preferred_element_type=jnp.float32) * scale
    local_top = jnp.max(wide, axis=-1)
    top = lax.pmax(local_top, "seq")
    total = lax.psum(jnp.sum(jnp.exp(wide - top[..., None]), axis=-1), "seq")
    glob_probs = jnp.exp(wide - top[..., None]) / total[..., None]
    glob_weights = glob_probs.astype(jnp.bfloat16)
    glob_part = jnp.einsum("hgt,thd->ghd", glob_weights, value3, preferred_element_type=jnp.float32)
    glob_out = lax.psum(glob_part, "seq").astype(jnp.bfloat16)
    attended = sparse_out.astype(jnp.bfloat16).at[target].set(glob_out, mode="drop")
    glob_mask = jnp.zeros((tokens,), jnp.bool_).at[target].set(True, mode="drop")
    sparse_grad = jnp.where(
        glob_mask[:, None, None],
        jnp.zeros_like(out_grad.reshape(tokens, heads, HD)),
        out_grad.reshape(tokens, heads, HD),
    )
    delta = jnp.sum(sparse_grad.astype(jnp.float32) * attended.astype(jnp.float32), axis=-1)
    grad_query, grad_window, grad_far, grad_wide = lax.map(
        partial(backward_group, global_rows=global_rows, scale=scale),
        (
            grouped(query_blocks),
            grouped(window),
            grouped(far_rows),
            grouped(window_valid),
            grouped(global_keep),
            grouped(sparse_grad.reshape(blocks, BLK, heads, HD)),
            grouped(delta.reshape(blocks, BLK, heads)),
        ),
    )
    grad_query = grad_query.reshape(tokens, heads, HD)
    grad_window = grad_window.reshape(blocks, 3, BLK, heads, 2 * HD)
    grad_wide = jnp.sum(grad_wide, axis=0)
    folded = jnp.zeros((blocks + 2, BLK, heads, 2 * HD), jnp.float32)
    folded = (
        folded.at[0:blocks]
        .add(grad_window[:, 0])
        .at[1 : blocks + 1]
        .add(grad_window[:, 1])
        .at[2 : blocks + 2]
        .add(grad_window[:, 2])
    )
    from_right = from_behind(folded[0], "seq", -1)
    from_left = from_behind(folded[blocks + 1], "seq", 1)
    local_pair = folded[1 : blocks + 1]
    local_pair = local_pair.at[blocks - 1].add(from_right).at[0].add(from_left)
    far_terms = jnp.transpose(grad_far.reshape(blocks, RAND, BLK, heads, 2 * HD), (0, 1, 3, 2, 4))
    outgoing = (
        jnp.zeros((devices, heads, capacity, BLK, 2 * HD), jnp.bfloat16)
        .at[owner_order, head_order, slot_order]
        .set(far_terms)
    )
    returned = lax.all_to_all(outgoing, "seq", split_axis=0, concat_axis=0, tiled=True)
    landing = jnp.where(asked >= 0, asked, blocks)
    gathered = (
        jnp.zeros((blocks, heads, BLK, 2 * HD), jnp.float32)
        .at[landing, jnp.arange(heads)[None, :, None]]
        .add(returned.astype(jnp.float32), mode="drop")
    )
    pair_grad = local_pair.reshape(tokens, heads, 2 * HD) + jnp.transpose(
        gathered, (0, 2, 1, 3)
    ).reshape(tokens, heads, 2 * HD)
    glob_attended = glob_out.astype(jnp.float32)
    glob_delta = jnp.sum(glob_grad.astype(jnp.float32) * glob_attended, axis=-1)
    glob_dot = jnp.einsum("ghd,thd->hgt", glob_grad, value3, preferred_element_type=jnp.float32)
    glob_dscore = (glob_probs * (glob_dot - jnp.transpose(glob_delta)[..., None])).astype(
        jnp.bfloat16
    )
    query_part = scale * jnp.einsum(
        "hgt,thd->ghd", glob_dscore, key3, preferred_element_type=jnp.float32
    )
    key_from_glob = scale * jnp.einsum(
        "hgt,ghd->thd", glob_dscore, glob_query, preferred_element_type=jnp.float32
    )
    value_from_glob = jnp.einsum(
        "hgt,ghd->thd", glob_weights, glob_grad, preferred_element_type=jnp.float32
    )
    summed = lax.psum((query_part, grad_wide), "seq")
    grad_query = grad_query.at[target].add(summed[0], mode="drop")
    pair_grad = pair_grad.at[target].add(summed[1], mode="drop")
    grad_key = pair_grad[..., :HD] + key_from_glob
    grad_value = pair_grad[..., HD:] + value_from_glob
    return (
        attended.reshape(tokens, heads * HD),
        grad_query.reshape(tokens, heads * HD).astype(jnp.bfloat16),
        grad_key.reshape(tokens, heads * HD).astype(jnp.bfloat16),
        grad_value.reshape(tokens, heads * HD).astype(jnp.bfloat16),
    )


BIG = 1e30
LIMIT = 63 * 1024 * 1024
NT = (((1,), (1,)), ((), ()))
TN = (((0,), (0,)), ((), ()))
NN = (((1,), (0,)), ((), ()))


def mm(left, right, dims):
    return lax.dot_general(left, right, dims, preferred_element_type=jnp.float32)


def head_kernel(
    n, tokens, q_hbm, k_hbm, v_hbm, g_hbm, rb_hbm, gp_hbm, att_ref, dq_ref, dk_ref, dv_ref,
    q_ref, k_ref, v_ref, g_ref, rb_ref, gp_ref, kq_send, v_send, g_send, tab_send, kq, vp, gp, tab,
    att_send, dv_send, dq_send, dk_send, att, dv, dq, dk,
    ka, qa, va, ga, probs, weights, dscore, load_sem, turn, send_sem, recv_sem,
):
    me = lax.axis_index("seq")
    total = n * tokens
    part = tokens // 2
    qb = tokens // BLK
    scale = 1.0 / math.sqrt(HD)
    half = me // 2
    inner = (me % 3 + 1) // 2
    near, far, mate = 2 - 2 * half, 3 - 2 * half, 1 - me + 4 * half
    others = [
        inner * mate + (1 - inner) * near,
        inner * near + (1 - inner) * far,
        inner * far + (1 - inner) * mate,
    ]

    barrier = pltpu.get_barrier_semaphore()
    for peer in others:
        pl.semaphore_signal(
            barrier, inc=1, device_id={"seq": peer}, device_id_type=pl.DeviceIdType.MESH
        )
    loads = [
        pltpu.make_async_copy(hbm, vmem, load_sem.at[i])
        for i, (hbm, vmem) in enumerate(
            ((k_hbm, k_ref), (q_hbm, q_ref), (v_hbm, v_ref), (g_hbm, g_ref), (rb_hbm, rb_ref), (gp_hbm, gp_ref))
        )
    ]
    for i in (4, 0, 1, 2, 3, 5):
        loads[i].start()

    stages = (
        (tab_send, tab), (kq_send, kq), (v_send, vp), (g_send, gp),
        (att_send, att), (dv_send, dv), (dq_send, dq), (dk_send, dk),
    )

    def copy(stage, peer, slot):
        send, recv = stages[stage]
        return pltpu.make_async_remote_copy(
            src_ref=send.at[peer],
            dst_ref=recv.at[slot],
            send_sem=send_sem.at[stage, peer],
            recv_sem=recv_sem.at[stage, slot],
            device_id={"seq": peer},
            device_id_type=pl.DeviceIdType.MESH,
        )

    def start(stage, peer):
        copy(stage, peer, me).start()

    def arrive(stage):
        for peer in others:
            copy(stage, peer, peer).wait_recv()

    def keep(stage):
        send, recv = stages[stage]
        recv[me] = send[me]

    def fold(ref, slot, rows):
        ref[slot, :, 0:HD] = rows[0:part]
        ref[slot, :, HD : 2 * HD] = rows[part:tokens]

    def fold_t(ref, slot, columns):
        stacked = jnp.concatenate([columns[:, 0:part], columns[:, part:tokens]], axis=0)
        ref[slot] = stacked.T.astype(jnp.bfloat16)

    lane = lax.broadcasted_iota(jnp.int32, (1, 128), 1)
    loads[4].wait()
    for h in range(n):
        mark = jnp.zeros((1, 128), jnp.int32)
        for r in range(RAND):
            for b in range(qb):
                at = lax.rem(HD + r * 8 * n + 8 * me + b, 128)
                mark = jnp.where(lane == at, rb_ref[r, h, b], mark)
        tab_send[h] = mark
    loads[0].wait()
    loads[1].wait()
    for h in range(n):
        cols = slice(h * HD, (h + 1) * HD)
        kq_send[h, :, 0:HD] = k_ref[:, cols]
        kq_send[h, :, HD : 2 * HD] = q_ref[:, cols] * jnp.bfloat16(scale)
    pl.semaphore_wait(barrier, n - 1)
    @pl.when(inner == 1)
    def _():
        for peer in (near, far, mate):
            start(0, peer)
            start(1, peer)

    loads[2].wait()
    for h in range(n):
        fold(v_send, h, v_ref[:, h * HD : (h + 1) * HD])
    loads[3].wait()
    for h in range(n):
        fold(g_send, h, g_ref[:, h * HD : (h + 1) * HD])

    @pl.when(inner == 1)
    def _():
        for stage in (2, 3):
            for peer in others:
                start(stage, peer)
        copy(1, mate, me).wait_send()
        pl.semaphore_signal(turn, inc=1, device_id={"seq": mate}, device_id_type=pl.DeviceIdType.MESH)

    pos = lax.broadcasted_iota(jnp.int32, (total, 128), 0)
    col = lax.broadcasted_iota(jnp.int32, (total, 128), 1)
    loads[5].wait()
    globals_here = gp_ref.shape[1]
    spots = lax.broadcasted_iota(jnp.int32, (total, globals_here), 0) == gp_ref[...]
    spread = mm(
        jnp.where(spots, 1.0, 0.0).astype(jnp.bfloat16),
        jnp.ones((globals_here, 128), jnp.bfloat16),
        NN,
    )
    is_global = spread > 0.5
    slot = col - HD
    block = (slot // 8) * qb + slot % 8
    mine = (slot >= 0) & (slot < 8 * n) & (slot % 8 < qb)
    key_block = pos // BLK
    window = mine & (block - key_block <= 1) & (key_block - block <= 1)
    open_key = window | is_global
    hot = jnp.where(mine & (block == key_block) & jnp.logical_not(is_global), 1.0, 0.0)

    @pl.when(inner == 0)
    def _():
        pl.semaphore_wait(turn, 1)
        for stage in (0, 1, 2):
            for peer in others:
                start(stage, peer)

    for stage in range(4):
        keep(stage)

    @pl.when(inner == 0)
    def _():
        copy(2, far, me).wait_send()
        for peer in others:
            start(3, peer)

    arrive(0)
    picks = tab[0]
    for c in range(1, n):
        picks = picks + tab[c]
    for r in range(RAND):
        shifted = picks if r == 0 else pltpu.roll(picks, 128 - r * 8 * n, 1)
        open_key = open_key | (mine & (key_block == shifted))
    bias = jnp.where(open_key, 0.0, -BIG).astype(jnp.bfloat16)
    arrive(1)
    pair = kq[...].reshape(total, 128)
    ka[...] = bias
    ka[:, 0:HD] = pair[:, 0:HD]
    qa[...] = hot.astype(jnp.bfloat16)
    qa[:, 0:HD] = pair[:, HD : 2 * HD]

    keys = ka[...]
    for a in range(n):
        score = mm(keys, qa[a * tokens : (a + 1) * tokens, :], NT)
        top = jnp.max(score, axis=0, keepdims=True)
        raised = jnp.exp(score - top)
        prob = raised * (1.0 / jnp.sum(raised, axis=0, keepdims=True))
        probs[a] = prob
        weights[a] = prob.astype(jnp.bfloat16)
    keys_t = keys[:, 0:HD].T

    order = others + [me]
    arrive(2)
    for c in range(n):
        va[c * tokens : c * tokens + part, :] = vp[c, :, 0:HD]
        va[c * tokens + part : (c + 1) * tokens, :] = vp[c, :, HD : 2 * HD]
    values = va[...]
    values_t = values.T
    outs = []
    for a in order:
        out = mm(values_t, weights[a], NN)
        fold_t(att_send, a, out)
        if a is not me and a is not others[2]:
            start(4, a)
        outs.append(out.astype(jnp.bfloat16).astype(jnp.float32))

    arrive(3)
    for c in range(n):
        ga[c, 0:part, :] = gp[c, :, 0:HD]
        ga[c, part:tokens, :] = gp[c, :, HD : 2 * HD]

    def value_grad(a):
        rows = pl.ds(pl.multiple_of(a * tokens, tokens), tokens)
        grad = jnp.zeros((tokens, HD), jnp.float32)
        for c in range(n):
            grad = grad + mm(weights[c, rows, :], ga[c], NN)
        fold(dv_send, a, grad.astype(jnp.bfloat16))

    def score_grad(a, out):
        grad = ga[a]
        delta = jnp.sum(grad.astype(jnp.float32).T * out, axis=0, keepdims=True)
        dprob = mm(values, grad, NT)
        dscore[a] = (probs[a] * (dprob - delta)).astype(jnp.bfloat16)

    def query_grad(a):
        fold_t(dq_send, a, mm(keys_t, dscore[a], NN) * scale)

    def key_grad(a):
        rows = pl.ds(pl.multiple_of(a * tokens, tokens), tokens)
        grad = jnp.zeros((tokens, HD), jnp.float32)
        for c in range(n):
            grad = grad + mm(dscore[c, rows, :], qa[c * tokens : (c + 1) * tokens, 0:HD], NN)
        fold(dk_send, a, grad.astype(jnp.bfloat16))

    value_grad(order[0])
    start(5, order[0])
    value_grad(order[1])
    start(5, order[1])
    score_grad(order[0], outs[0])
    query_grad(order[0])
    start(6, order[0])
    score_grad(order[1], outs[1])
    score_grad(order[2], outs[2])
    score_grad(order[3], outs[3])
    key_grad(order[0])
    start(7, order[0])
    query_grad(order[1])
    start(6, order[1])
    key_grad(order[1])
    start(7, order[1])
    start(4, order[2])
    value_grad(order[2])
    start(5, order[2])
    query_grad(order[2])
    start(6, order[2])
    key_grad(order[2])
    start(7, order[2])
    value_grad(order[3])
    query_grad(order[3])
    key_grad(order[3])
    for stage in range(4, 8):
        keep(stage)

    def unpack(stage, ref):
        recv = stages[stage][1]
        for h in range(n):

            @pl.when(me != h)
            def _():
                copy(stage, h, h).wait_recv()

            cols = slice(h * HD, (h + 1) * HD)
            ref[0:part, cols] = recv[h, :, 0:HD]
            ref[part:tokens, cols] = recv[h, :, HD : 2 * HD]

    for stage, ref in ((4, att_ref), (5, dv_ref), (6, dq_ref)):
        unpack(stage, ref)
    @pl.when(inner == 1)
    def _():
        copy(2, far, me).wait_send()

    @pl.when(inner == 0)
    def _():
        copy(1, mate, me).wait_send()

    for stage in range(7):
        for peer in (near, far) if stage == 1 else (mate, near) if stage == 2 else others:
            copy(stage, peer, me).wait_send()
    unpack(7, dk_ref)
    for peer in others:
        copy(7, peer, me).wait_send()


def write_out(*refs):
    count = len(refs) // 2
    sources, targets, sem = refs[:count], refs[count : 2 * count], refs[-1]
    stores = [pltpu.make_async_copy(sources[i], targets[i], sem.at[i]) for i in range(count)]
    for store in stores:
        store.start()
    for store in stores:
        store.wait()


def local_heads(query_rows, key_rows, value_rows, out_grad, random_blocks, global_positions):
    tokens, width = query_rows.shape
    n = lax.axis_size("seq")
    total = n * tokens
    bf16, f32 = jnp.bfloat16, jnp.float32
    where_it_lies = pl.BlockSpec(memory_space=pltpu.HBM)
    rows = [pltpu.VMEM((tokens, width), bf16)] * 4
    whole = pltpu.VMEM((n, tokens, 2 * HD), bf16)
    folded = pltpu.VMEM((n, tokens // 2, 2 * HD), bf16)
    small = pltpu.VMEM((n, 1, 128), jnp.int32)
    results = pl.pallas_call(
        partial(head_kernel, n, tokens),
        out_shape=[pltpu.VMEM((tokens, width), bf16)] * 4,
        in_specs=[where_it_lies] * 6,
        out_specs=[pl.BlockSpec(memory_space=pltpu.VMEM)] * 4,
        scratch_shapes=[
            *rows,
            pltpu.SMEM((RAND,) + random_blocks.shape[:2], jnp.int32),
            pltpu.VMEM((1, global_positions.shape[0]), jnp.int32),
            whole, folded, folded, small,
            whole, folded, folded, small,
            *([folded] * 8),
            pltpu.VMEM((total, 128), bf16),
            pltpu.VMEM((total, 128), bf16),
            pltpu.VMEM((total, HD), bf16),
            pltpu.VMEM((n, tokens, HD), bf16),
            pltpu.VMEM((n, total, tokens), f32),
            pltpu.VMEM((n, total, tokens), bf16),
            pltpu.VMEM((n, total, tokens), bf16),
            pltpu.SemaphoreType.DMA((6,)),
            pltpu.SemaphoreType.REGULAR,
            pltpu.SemaphoreType.DMA((8, n)),
            pltpu.SemaphoreType.DMA((8, n)),
        ],
        compiler_params=pltpu.CompilerParams(
            collective_id=0, has_side_effects=True, vmem_limit_bytes=LIMIT
        ),
        cost_estimate=pl.CostEstimate(
            flops=14 * total * total * HD, bytes_accessed=16 * tokens * width, transcendentals=total * total
        ),
    )(
        query_rows, key_rows, value_rows, out_grad,
        jnp.transpose(random_blocks, (2, 0, 1)), global_positions.reshape(1, -1),
    )
    return pl.pallas_call(
        write_out,
        out_shape=[jax.ShapeDtypeStruct((tokens, width), bf16)] * 4,
        in_specs=[pl.BlockSpec(memory_space=pltpu.VMEM)] * 4,
        out_specs=[where_it_lies] * 4,
        scratch_shapes=[pltpu.SemaphoreType.DMA((4,))],
    )(*(pltpu.with_memory_space_constraint(r, pltpu.VMEM) for r in results))


def local(query_rows, key_rows, value_rows, out_grad, random_blocks, global_positions):
    n = lax.axis_size("seq")
    tokens = query_rows.shape[0]
    one_head_each = query_rows.shape[1] == n * HD and n > 1
    fits = n == 4 and 8 * n <= 128 - HD and tokens // BLK <= 8 and n * tokens // BLK <= 128
    if one_head_each and fits and tokens % 256 == 0 and n * tokens <= 1024:
        run = local_heads
    else:
        run = local_wide
    return run(query_rows, key_rows, value_rows, out_grad, random_blocks, global_positions)


def solution(mesh):
    placed = (
        P(("groups", "seq"), ("head", "pair")),
        P(("groups", "seq"), ("head", "pair")),
        P(("groups", "seq"), ("head", "pair")),
        P(("groups", "seq"), ("head", "pair")),
        P(("groups", "head", "pair"), "seq", None),
        P("groups"),
    )
    return jax.shard_map(
        local,
        mesh=mesh,
        in_specs=placed,
        out_specs=(
            P(("groups", "seq"), ("head", "pair")),
            P(("groups", "seq"), ("head", "pair")),
            P(("groups", "seq"), ("head", "pair")),
            P(("groups", "seq"), ("head", "pair")),
        ),
        check_vma=False,
    )
```
